512 devices in a mesh: dp: 32 (over y, x), ctx: 16 (over z, core).
Axes of the slice: x: 4, y: 8, z: 8, core: 2. Of those that a mesh axis runs over, the one named last changes fastest.
Arguments:
- queries: bfloat16 [32, 2048, 4096], P('dp', 'ctx'), may hold values from -8 to 8
- keys: bfloat16 [32, 2048, 1024], P('dp', 'ctx'), may hold values from -8 to 8
- values: bfloat16 [32, 2048, 1024], P('dp', 'ctx'), may hold values from -6 to 6
- grad_out: bfloat16 [32, 2048, 4096], P('dp', 'ctx'), may hold values from -16 to 16
- sink_logit: float32 [32], P('ctx'), may hold values from 1 to 4
- doc_lengths: int32 [32, 16], P('dp'), may hold values from 1 to 256, 2048 in all within a row
- slab_order: int32 [32, 32], P('dp'), may hold values from 0 to 31, each once within a row
Outputs:
- grad_queries: bfloat16 [32, 2048, 4096], P('dp', 'ctx')
- grad_keys: bfloat16 [32, 2048, 1024], P('dp', 'ctx')
- grad_values: bfloat16 [32, 2048, 1024], P('dp', 'ctx')
- grad_sink: float32 [32], P('ctx')
The draws below stay inside these ranges and needn't reach their ends.
Inputs may be any that keep to these rules, and one draw needn't show every extreme that they name: `doc_lengths`: the longest document has exactly 256 tokens. `slab_order`: each row is a permutation of the slabs.
All inputs are finite; a program needn't handle non-finite values.
Results may differ from the reference program's by a relative error of at most 0.02.
Values may be sent and summed in bfloat16 or wider, within the bound.
A program may use at most 64 MiB of HBM per device.

```python
import math
import jax
import jax.numpy as jnp
import numpy as np
from jax import lax

HD = 128
HQ = 32
HK = 8
SEQ = 2048
SLABS = 32
DOC_MOST = 256
DOCS = 16
N_DP = 32


def draw_queries(key, part):
    key = jax.random.fold_in(key, 11)
    drawn = jax.random.normal(key, (N_DP, SEQ, HQ * HD), jnp.float32)
    return jnp.clip(drawn, -8.0, 8.0).astype(jnp.bfloat16)


def draw_keys(key, part):
    key = jax.random.fold_in(key, 17)
    drawn = jax.random.normal(key, (N_DP, SEQ, HK * HD), jnp.float32)
    return jnp.clip(drawn, -8.0, 8.0).astype(jnp.bfloat16)


def draw_grad_out(key, part):
    key = jax.random.fold_in(key, 29)
    groups = jnp.arange(N_DP, dtype=jnp.float32)
    rising = 1.0 + 2.0 * groups / max(N_DP - 1, 1)
    drawn = jax.random.normal(key, (N_DP, SEQ, HQ * HD), jnp.float32)
    return jnp.clip(drawn * rising[:, None, None], -16.0, 16.0).astype(jnp.bfloat16)


def shard_levels(rng, dims, cuts, least, high):
    factor_of = 1.0
    for position, shards_of in cuts:
        draws = jax.random.uniform(jax.random.fold_in(jax.random.fold_in(rng, 6), position), (shards_of,), jnp.float32, least / len(cuts), high / len(cuts))
        factor_of = factor_of * jnp.repeat(jnp.exp(draws), dims[position] // shards_of).reshape((-1,) + (1,) * (len(dims) - 1 - position))
    return factor_of


def split_up(count, total, bound, lean):
    loads = [(1 << 20) // math.isqrt(rank ** lean) + 1 for rank in range(2, count + 1)]
    spare, counts = total - bound - (count - 1), [1] * (count - 1)
    while spare > 0:
        free = [i for i in range(count - 1) if counts[i] < bound]
        mass, left = sum([loads[i] for i in free]), spare
        for i in free:
            more = min(bound - counts[i], max(1, left * loads[i] // mass), spare)
            counts[i] = counts[i] + more
            spare = spare - more
    return np.array([bound] + counts)


def ragged(key, amount, total, bound, slope):
    if amount == 2:
        one = jax.random.randint(key, (), max(1, total - bound), min(bound, total - 1) + 1)
        return jnp.stack([one, total - one])
    sizes = jnp.asarray(split_up(amount, total, bound, slope), jnp.int32)
    couples = (amount - 1) // 2
    giver, taker = sizes[1:1 + 2 * couples:2], sizes[2:2 + 2 * couples:2]
    slack = jnp.minimum(giver - 1, bound - taker)
    moved = jax.random.randint(jax.random.fold_in(key, 1), (couples,), 0, 1 << 20) % (slack + 1)
    sizes = sizes.at[1:1 + 2 * couples:2].set(giver - moved).at[2:2 + 2 * couples:2].set(taker + moved)
    return sizes[jax.random.permutation(jax.random.fold_in(key, 2), amount)]


def bell_draw(rng, shape, spread, bound, pieces=(), held_as=jnp.bfloat16):
    values = jax.random.normal(rng, shape, jnp.float32) * spread
    if len(pieces) > 0:
        values = shard_levels(rng, shape, pieces, -0.22, 0.18) * values
    return jnp.clip(values, min=-bound, max=bound).astype(held_as)


def setup_inputs(seed: int = 0) -> dict:
    splits = jax.random.split(jax.random.key(seed), 8)
    return {
        "queries": draw_queries(jax.random.fold_in(splits[7], 71), 0),
        "keys": draw_keys(jax.random.fold_in(splits[7], 71), 0),
        "values": bell_draw(splits[2], (N_DP, SEQ, HK * HD), 1.0, 6.0, ((0, 32), (1, 16))),
        "grad_out": draw_grad_out(jax.random.fold_in(splits[7], 71), 0),
        "sink_logit": jnp.clip(1.0 + 3.0 * jax.random.uniform(splits[4], (HQ,), jnp.float32) ** shard_levels(splits[4], (HQ,), ((0, 16),), -0.2, 0.2), 1.0, 4.0),
        "doc_lengths": jax.vmap(lambda own: ragged(own, DOCS, SEQ, DOC_MOST, 2))(jax.random.split(splits[5], N_DP)).reshape((N_DP, DOCS)).astype(jnp.int32),
        "slab_order": jax.vmap(lambda own: jax.random.permutation(own, SLABS))(jax.random.split(splits[6], N_DP)).reshape((N_DP, SLABS)).astype(jnp.int32),
    }


masked_score = -1e+30

def doc_index(lengths, positions):
    doc_ends = jnp.cumsum(lengths)
    return lax.optimization_barrier(jnp.sum((positions[:, None] >= doc_ends[None, :]).astype(jnp.int32), axis=1))

def head_group(query_all, key_all, value_all, grad_all, sinks, lengths):
    seq_len, head_count, head_width = query_all.shape
    block_rows = min(512, seq_len)
    reach_rows = min(256, seq_len // 4)
    span_rows = block_rows + reach_rows
    factor = 1.0 / math.sqrt(head_width)
    doc_ids = doc_index(lengths, jnp.arange(seq_len, dtype=jnp.int32))
    pad_keys = jnp.concatenate([jnp.zeros((reach_rows, head_width), key_all.dtype), key_all], 0)
    pad_values = jnp.concatenate([jnp.zeros((reach_rows, head_width), value_all.dtype), value_all], 0)
    pad_docs = jnp.concatenate([jnp.full((reach_rows,), -1, jnp.int32), doc_ids.astype(jnp.int32)], 0)

    def one_block(totals, block_index):
        key_total, value_total = totals
        first_row = (block_index * block_rows).astype(jnp.int32)
        query_rows = lax.dynamic_slice_in_dim(query_all, first_row, block_rows, 0).astype(jnp.float32)
        grad_rows = lax.dynamic_slice_in_dim(grad_all, first_row, block_rows, 0).astype(jnp.float32)
        key_rows = lax.dynamic_slice_in_dim(pad_keys, first_row, span_rows, 0).astype(jnp.float32)
        value_rows = lax.dynamic_slice_in_dim(pad_values, first_row, span_rows, 0).astype(jnp.float32)
        query_doc = lax.dynamic_slice_in_dim(doc_ids, first_row, block_rows, 0)
        key_doc = lax.dynamic_slice_in_dim(pad_docs, first_row, span_rows, 0)
        query_place = first_row + jnp.arange(block_rows, dtype=jnp.int32)
        key_place = first_row - reach_rows + jnp.arange(span_rows, dtype=jnp.int32)
        allowed = (query_doc[:, None] == key_doc[None, :]) & (key_place[None, :] <= query_place[:, None])
        scores = jnp.einsum('bhd,kd->hbk', query_rows, key_rows) * factor
        scores = jnp.where(allowed[None], scores, masked_score)
        maxima = jnp.maximum(sinks[:, None], lax.optimization_barrier(jnp.max(scores, axis=2)))
        weights = jnp.exp(scores - maxima[:, :, None])
        sink_weight = jnp.exp(sinks[:, None] - maxima)
        row_total = sink_weight + lax.optimization_barrier(jnp.sum(weights, axis=2))
        softmax = weights / row_total[:, :, None]
        sink_share = sink_weight / row_total
        rounded = softmax.astype(jnp.bfloat16)
        attended = jnp.einsum('hbk,kd->bhd', rounded.astype(jnp.float32), value_rows).astype(jnp.bfloat16)
        row_delta = lax.optimization_barrier(jnp.sum(grad_rows * attended.astype(jnp.float32), axis=2)).T
        grad_prob = jnp.einsum('bhd,kd->hbk', grad_rows, value_rows)
        grad_score = (softmax * (grad_prob - row_delta[:, :, None])).astype(jnp.bfloat16)
        query_grad = (jnp.einsum('hbk,kd->bhd', grad_score.astype(jnp.float32), key_rows) * factor).astype(jnp.bfloat16)
        key_grad = jnp.einsum('hbk,bhd->kd', grad_score.astype(jnp.float32), query_rows) * factor
        value_grad = jnp.einsum('hbk,bhd->kd', rounded.astype(jnp.float32), grad_rows)
        key_total = lax.dynamic_update_slice_in_dim(key_total, lax.dynamic_slice_in_dim(key_total, first_row, span_rows, 0) + key_grad, first_row, 0)
        value_total = lax.dynamic_update_slice_in_dim(value_total, lax.dynamic_slice_in_dim(value_total, first_row, span_rows, 0) + value_grad, first_row, 0)
        sink_part = -lax.optimization_barrier(jnp.sum(sink_share * row_delta, axis=1))
        return ((key_total, value_total), (query_grad, sink_part))
    initial = (jnp.zeros((reach_rows + seq_len, head_width), jnp.float32), jnp.zeros((reach_rows + seq_len, head_width), jnp.float32))
    (key_total, value_total), (query_grad, sink_parts) = lax.scan(one_block, initial, jnp.arange(seq_len // block_rows, dtype=jnp.int32))
    return (query_grad.reshape(seq_len, head_count, head_width), key_total[reach_rows:], value_total[reach_rows:], lax.optimization_barrier(jnp.sum(sink_parts, axis=0)))

def inverse_of(slab_ids):
    count = slab_ids.shape[0]
    column = jnp.arange(count, dtype=jnp.int32)
    return lax.optimization_barrier(jnp.sum(jnp.where(slab_ids[:, None] == column[None, :], column[:, None], 0), axis=0)).astype(jnp.int32)

def to_natural(rows, inverse):
    count = inverse.shape[0]
    return rows.reshape(count, rows.shape[0] // count, rows.shape[1])[inverse].reshape(rows.shape)

def to_stored(rows, slab_ids):
    count = slab_ids.shape[0]
    return rows.reshape(count, rows.shape[0] // count, rows.shape[1])[slab_ids].reshape(rows.shape)

def reference(queries, keys, values, grad_out, sink_logit, doc_lengths, slab_order):
    shared = HQ // HK

    def per_group(group_items):
        query_seq, key_seq, value_seq, grad_seq, lengths, slab_ids = group_items
        inverse = inverse_of(slab_ids)
        query_nat = to_natural(query_seq, inverse).reshape(SEQ, HK, shared, HD)
        grad_nat = to_natural(grad_seq, inverse).reshape(SEQ, HK, shared, HD)
        key_nat = to_natural(key_seq, inverse).reshape(SEQ, HK, HD)
        value_nat = to_natural(value_seq, inverse).reshape(SEQ, HK, HD)

        def per_head(head_index):
            sinks = lax.dynamic_slice_in_dim(sink_logit, head_index * shared, shared)
            return head_group(query_nat[:, head_index], key_nat[:, head_index], value_nat[:, head_index], grad_nat[:, head_index], sinks, lengths)
        query_grad, key_grad, value_grad, sink_grad = lax.map(per_head, jnp.arange(HK, dtype=jnp.int32))
        query_grad = query_grad.transpose(1, 0, 2, 3).reshape(SEQ, HQ * HD)
        key_grad = key_grad.transpose(1, 0, 2).reshape(SEQ, HK * HD).astype(jnp.bfloat16)
        value_grad = value_grad.transpose(1, 0, 2).reshape(SEQ, HK * HD).astype(jnp.bfloat16)
        return (to_stored(query_grad, slab_ids), to_stored(key_grad, slab_ids), to_stored(value_grad, slab_ids), sink_grad.reshape(HQ))
    grad_queries, grad_keys, grad_values, sink_terms = lax.map(per_group, (queries, keys, values, grad_out, doc_lengths, slab_order))
    return (grad_queries, grad_keys, grad_values, lax.optimization_barrier(jnp.sum(sink_terms, axis=0)))
```

```python
import functools
import math

import jax
import jax.numpy as jnp
from jax import lax
from jax.experimental import pallas as pl
from jax.experimental.pallas import tpu as pltpu
from jax.sharding import PartitionSpec as P

HD = 128
SLAB = 64
REACH = 4
WIN = REACH + 1
FAR = -1e30
MESH = pl.DeviceIdType.MESH
F32 = jnp.float32
BF16 = jnp.bfloat16


def kernel(n_dp, n_ctx, order, lens, sink, q_hbm, k_hbm, v_hbm, g_hbm,
           gq_out, gk_out, gv_out, gs_out,
           kv0, kv1, kv2, kv3, q_buf, g_buf, gq_buf, terms, part, inbox, bias, fin,
           sink_own, sink_in, gs_own, gs_in, window, slot,
           load_sem, swap_send, swap_recv, qg_load, qg_send, qg_recv,
           ag_send, ag_recv, rs_send, rs_recv, gq_store, gq_send, gq_recv,
           fin_store, fin_send, fin_recv, s_send, s_recv, t_send, t_recv):
    kvs = (kv0, kv1, kv2, kv3)
    n_heads = len(kvs)
    n_z = n_ctx // 2
    per_chip = 4
    n_slabs = n_z * per_chip
    dp, ctx = lax.axis_index("dp"), lax.axis_index("ctx")
    z, core = ctx // 2, ctx % 2
    peer = 2 * z + 1 - core
    right = 2 * lax.rem(z + 1, n_z) + core
    left = 2 * lax.rem(z + n_z - 1, n_z) + core
    half = n_z // 2

    def xor(value, bit):
        return value + bit - 2 * bit * lax.rem(value // bit, 2)

    ctx_bits = [1 << i for i in range(n_ctx.bit_length() - 1)]
    dp_bits = [1 << i for i in range(n_dp.bit_length() - 1)]
    ctx_mates = [(dp, xor(ctx, bit)) for bit in ctx_bits]
    dp_mates = [(xor(dp, bit), ctx) for bit in dp_bits]

    barrier = pltpu.get_barrier_semaphore()
    greeted = [(dp, left), (dp, right)] + ctx_mates + dp_mates
    for mate in greeted:
        pl.semaphore_signal(barrier, inc=1, device_id=mate, device_id_type=MESH)

    wide = q_hbm.shape[2] // 2
    kw = k_hbm.shape[2] // 2
    mine = pl.ds(2 * ctx, 2)
    loads = []
    for k in range(n_heads):
        cols = pl.ds(pl.multiple_of(core * kw + k * HD, HD), HD)
        for t, src in enumerate((k_hbm, v_hbm)):
            copy = pltpu.make_async_copy(src.at[:, :, cols], kvs[k].at[t, mine], load_sem.at[k, t])
            copy.start()
            loads.append(copy)
    own_cols = pl.ds(pl.multiple_of(core * wide, HD), wide)
    peer_cols = pl.ds(pl.multiple_of((1 - core) * wide, HD), wide)
    own_rows = pl.ds(2 * core, 2)
    qg_loads = []
    for t, (src, dst) in enumerate(((q_hbm, q_buf), (g_hbm, g_buf))):
        copy = pltpu.make_async_copy(src.at[:, :, own_cols], dst.at[own_rows], qg_load.at[t])
        copy.start()
        qg_loads.append(copy)
    lane = lax.broadcasted_iota(jnp.int32, (1, HD), 1)
    sink_own[...] = jnp.zeros_like(sink_own)
    sink_own[pl.ds(ctx, 1), :] = jnp.where(lane < SLAB, sink[0], sink[1])

    pl.semaphore_wait(barrier, len(greeted))

    swaps = []
    for k in range(n_heads):
        cols = pl.ds(pl.multiple_of((1 - core) * kw + k * HD, HD), HD)
        for t, src in enumerate((k_hbm, v_hbm)):
            copy = pltpu.make_async_remote_copy(
                src.at[:, :, cols], kvs[k].at[t, mine], swap_send.at[k, t], swap_recv.at[k, t],
                device_id=(dp, peer), device_id_type=MESH)
            copy.start()
            swaps.append(copy)

    def chip_rows(z_of):
        return pl.ds(per_chip * z_of, per_chip)

    def gather(k, way, step):
        owner = lax.rem(z - (step - 1) + n_z, n_z) if way == 0 else lax.rem(z + step - 1, n_z)
        block = kvs[k].at[:, chip_rows(owner)] if step < half else kvs[k].at[way, chip_rows(owner)]
        return pltpu.make_async_remote_copy(
            block, block, ag_send.at[k, way, step - 1], ag_recv.at[k, way, step - 1],
            device_id=(dp, (right, left)[way]), device_id_type=MESH)

    for k in range(n_heads):
        for t in range(2):
            loads[2 * k + t].wait()
            swaps[2 * k + t].wait_recv()
        for way in range(2):
            gather(k, way, 1).start()

    qg_swaps = []
    for t, (src, dst) in enumerate(((q_hbm, q_buf), (g_hbm, g_buf))):
        copy = pltpu.make_async_remote_copy(
            src.at[:, :, peer_cols], dst.at[own_rows], qg_send.at[t], qg_recv.at[t],
            device_id=(dp, peer), device_id_type=MESH)
        copy.start()
        qg_swaps.append(copy)

    def exchange(own, slots, send, recv, at, mate):
        copy = pltpu.make_async_remote_copy(
            own, slots.at[at], send.at[at], recv.at[at], device_id=mate, device_id_type=MESH)
        copy.start()
        copy.wait()
        own[...] = own[...] + slots[at]

    places = [order[0, 4 * z + i] for i in range(per_chip)]
    for i in range(per_chip):
        for w in range(WIN):
            window[i * WIN + w] = 0

    def note_slab(j, carry):
        place = order[0, j]
        new = []
        for i in range(per_chip):
            w = place - places[i] + REACH
            slot[j * per_chip + i] = jnp.where((w >= 0) & (w < WIN), i * WIN + w, per_chip * WIN)
            for v in range(WIN):
                new.append(jnp.where(w == v, j, carry[i * WIN + v]))
        return tuple(new)

    found = lax.fori_loop(0, n_slabs, note_slab, (jnp.int32(0),) * (per_chip * WIN))
    for i in range(per_chip * WIN):
        window[i] = found[i]

    row = lax.rem(lane, SLAB)
    key = lax.broadcasted_iota(jnp.int32, (WIN * SLAB, HD), 0)
    for i in range(per_chip):
        here = places[i] * SLAB + row
        begin = jnp.zeros_like(here)
        end = jnp.int32(0)
        for d in range(lens.shape[1]):
            end = end + lens[0, d]
            begin = jnp.where(here >= end, end, begin)
        begin = begin - (places[i] - REACH) * SLAB
        allowed = (key >= begin) & (key <= row + REACH * SLAB)
        bias[i] = jnp.where(allowed, 0.0, FAR)

    for k in range(n_heads):
        terms[k, per_chip * WIN] = jnp.zeros_like(terms[k, per_chip * WIN])
    gs_own[...] = jnp.zeros_like(gs_own)

    for step in range(2, half + 1):
        for k in range(n_heads):
            for way in range(2):
                gather(k, way, step - 1).wait_recv()
                gather(k, way, step).start()
        if step == 2:
            for at, mate in enumerate(ctx_mates):
                exchange(sink_own, sink_in, s_send, s_recv, at, mate)

    factor = 1.0 / math.sqrt(HD)
    group = wide // HD // n_heads

    def attend(k, i):
        kv = kvs[k]
        keys = jnp.concatenate([kv[0, window[i * WIN + w]] for w in range(WIN)], axis=0)
        vals = jnp.concatenate([kv[1, window[i * WIN + w]] for w in range(WIN)], axis=0)
        spans = [pl.ds((k * group + h) * HD, HD) for h in range(group)]
        q = jnp.concatenate([q_buf[i, :, span] for span in spans], axis=0)
        g = jnp.concatenate([g_buf[i, :, span] for span in spans], axis=0)
        pairs = group // 2
        first = pairs * (n_heads * core + k)
        sinks = jnp.concatenate([sink_own[pl.ds(first + p, 1), :] for p in range(pairs)], axis=1)
        nt = (((1,), (1,)), ((), ()))
        scores = lax.dot_general(keys, q, nt, preferred_element_type=F32)
        grad_prob = lax.dot_general(vals, g, nt, preferred_element_type=F32)
        mask = bias[i]
        scores = scores * factor + jnp.concatenate([mask] * pairs, axis=1)
        peak = jnp.maximum(sinks, jnp.max(scores, axis=0, keepdims=True))
        weights = jnp.exp(scores - peak)
        sink_weight = jnp.exp(sinks - peak)
        total = sink_weight + jnp.sum(weights, axis=0, keepdims=True)
        inverse = 1.0 / total
        softmax = weights * inverse
        rounded = softmax.astype(BF16)
        delta = jnp.sum(rounded.astype(F32) * grad_prob, axis=0, keepdims=True)
        grad_score = (softmax * (grad_prob - delta)).astype(BF16)
        grad_key = jnp.dot(grad_score, q, preferred_element_type=F32) * factor
        grad_val = jnp.dot(rounded, g, preferred_element_type=F32)
        grad_query = lax.dot_general(
            grad_score, keys, (((0,), (0,)), ((), ())), preferred_element_type=F32) * factor
        for h in range(group):
            gq_buf[i, :, spans[h]] = grad_query[h * SLAB:(h + 1) * SLAB].astype(BF16)
        for w in range(WIN):
            terms[k, i * WIN + w, 0] = grad_key[w * SLAB:(w + 1) * SLAB]
            terms[k, i * WIN + w, 1] = grad_val[w * SLAB:(w + 1) * SLAB]
        share = sink_weight * inverse * delta
        for p in range(pairs):
            at = pl.ds(first + p, 1)
            gs_own[at, :] = gs_own[at, :] - share[:, p * HD:(p + 1) * HD]

    def own_terms(k, j, t):
        total = terms[k, slot[j * per_chip], t]
        for i in range(1, per_chip):
            total = total + terms[k, slot[j * per_chip + i], t]
        return total

    def reduced(k, way, step):
        far = half + 1 - step
        owner = lax.rem(z - far + n_z, n_z) if way == 0 else lax.rem(z + far, n_z)
        src, dst = part.at[k, :, chip_rows(owner)], inbox.at[k, way, step - 1]
        if step == 1:
            src, dst = part.at[k, way, chip_rows(owner)], inbox.at[k, way, step - 1, way]
        return owner, pltpu.make_async_remote_copy(
            src, dst, rs_send.at[k, way, step - 1], rs_recv.at[k, way, step - 1],
            device_id=(dp, (left, right)[way]), device_id_type=MESH)

    def sum_and_send(k, way, step):
        owner, copy = reduced(k, way, step)
        if step > 1:
            reduced(k, way, step - 1)[1].wait_recv()
        tensors = (way,) if step == 1 else (0, 1)

        def one(j, carry):
            for t in tensors:
                total = own_terms(k, per_chip * owner + j, t)
                if step > 2 or (step == 2 and t == way):
                    total = total + inbox[k, way, step - 2, t, j].astype(F32)
                part[k, t, per_chip * owner + j] = total.astype(BF16)
            return carry

        lax.fori_loop(0, per_chip, one, 0)
        copy.start()

    def gq_copies(k):
        cols = pl.ds(pl.multiple_of(core * wide + k * group * HD, HD), group * HD)
        here = pl.ds(k * group * HD, group * HD)
        keep = pltpu.make_async_copy(
            gq_buf.at[own_rows, :, here], gq_out.at[:, :, cols], gq_store.at[k])
        away = pltpu.make_async_remote_copy(
            gq_buf.at[pl.ds(2 - 2 * core, 2), :, here], gq_out.at[:, :, cols],
            gq_send.at[k], gq_recv.at[k], device_id=(dp, peer), device_id_type=MESH)
        return keep, away

    for t in range(2):
        qg_loads[t].wait()
        qg_swaps[t].wait_recv()
    for k in range(n_heads):
        for way in range(2):
            gather(k, way, half).wait_recv()

        def one_slab(i, carry, k=k):
            attend(k, i)
            return carry

        lax.fori_loop(0, per_chip, one_slab, 0)
        for way in range(2):
            sum_and_send(k, way, 1)
        for copy in gq_copies(k):
            copy.start()

    mates = ctx_mates[1:] + dp_mates + ctx_mates[:1]
    left_over = list(enumerate(mates))
    for step in range(2, half + 1):
        for k in range(n_heads):
            for way in range(2):
                sum_and_send(k, way, step)
            if left_over:
                at, mate = left_over.pop(0)
                exchange(gs_own, gs_in, t_send, t_recv, at, mate)
    for at, mate in left_over:
        exchange(gs_own, gs_in, t_send, t_recv, at, mate)

    sums = gs_own[pl.ds(ctx, 1), :]
    gs_out[0] = jnp.sum(jnp.where(lane < SLAB, sums, 0.0))
    gs_out[1] = jnp.sum(jnp.where(lane < SLAB, 0.0, sums))

    def fin_copies(k):
        cols = pl.ds(pl.multiple_of(core * kw + k * HD, HD), HD)
        copies = []
        for t, out in enumerate((gk_out, gv_out)):
            keep = pltpu.make_async_copy(
                fin.at[k, t, own_rows], out.at[:, :, cols], fin_store.at[k, t])
            away = pltpu.make_async_remote_copy(
                fin.at[k, t, pl.ds(2 - 2 * core, 2)], out.at[:, :, cols],
                fin_send.at[k, t], fin_recv.at[k, t], device_id=(dp, peer), device_id_type=MESH)
            copies.append((keep, away))
        return copies

    for k in range(n_heads):
        for way in range(2):
            reduced(k, way, half)[1].wait_recv()

        def last(j, carry, k=k):
            for t in range(2):
                total = own_terms(k, per_chip * z + j, t)
                for way in range(2):
                    total = total + inbox[k, way, half - 1, t, j].astype(F32)
                fin[k, t, j] = total.astype(BF16)
            return carry

        lax.fori_loop(0, per_chip, last, 0)
        for keep, away in fin_copies(k):
            keep.start()
            away.start()

    for copy in swaps + qg_swaps:
        copy.wait_send()
    for k in range(n_heads):
        for way in range(2):
            for step in range(1, half + 1):
                gather(k, way, step).wait_send()
                reduced(k, way, step)[1].wait_send()
        keep, away = gq_copies(k)
        keep.wait()
        away.wait()
        for keep, away in fin_copies(k):
            keep.wait()
            away.wait()


def on_device(n_dp, n_ctx, queries, keys, values, grad_out, sink_logit, doc_lengths, slab_order):
    def slabs(x):
        return x.reshape(2, SLAB, x.shape[2])

    n_heads, n_z, per_chip = 4, n_ctx // 2, 4
    n_slabs = n_z * per_chip
    wide = queries.shape[2] // 2
    n_pairs = 16
    half = n_z // 2
    n_s, n_t = n_ctx.bit_length() - 1, n_ctx.bit_length() - 1 + n_dp.bit_length() - 1
    dma = pltpu.SemaphoreType.DMA
    any_spec = pl.BlockSpec(memory_space=pl.ANY)
    smem = pl.BlockSpec(memory_space=pltpu.SMEM)
    kv = pltpu.VMEM((2, n_slabs, SLAB, HD), BF16)
    rows = pltpu.VMEM((per_chip, SLAB, wide), BF16)
    gq, gk, gv, gs = pl.pallas_call(
        functools.partial(kernel, n_dp, n_ctx),
        out_shape=(
            jax.ShapeDtypeStruct((2, SLAB, queries.shape[2]), BF16),
            jax.ShapeDtypeStruct((2, SLAB, keys.shape[2]), BF16),
            jax.ShapeDtypeStruct((2, SLAB, keys.shape[2]), BF16),
            jax.ShapeDtypeStruct((2,), F32),
        ),
        in_specs=[smem] * 3 + [any_spec] * 4,
        out_specs=(any_spec, any_spec, any_spec, smem),
        scratch_shapes=[
            kv, kv, kv, kv, rows, rows, rows,
            pltpu.VMEM((n_heads, per_chip * WIN + 1, 2, SLAB, HD), F32),
            pltpu.VMEM((n_heads, 2, n_slabs, SLAB, HD), BF16),
            pltpu.VMEM((n_heads, 2, half, 2, per_chip, SLAB, HD), BF16),
            pltpu.VMEM((per_chip, WIN * SLAB, HD), F32),
            pltpu.VMEM((n_heads, 2, per_chip, SLAB, HD), BF16),
            pltpu.VMEM((n_pairs, HD), F32),
            pltpu.VMEM((n_s, n_pairs, HD), F32),
            pltpu.VMEM((n_pairs, HD), F32),
            pltpu.VMEM((n_t, n_pairs, HD), F32),
            pltpu.SMEM((per_chip * WIN,), jnp.int32),
            pltpu.SMEM((n_slabs * per_chip,), jnp.int32),
            dma((n_heads, 2)), dma((n_heads, 2)), dma((n_heads, 2)),
            dma((2,)), dma((2,)), dma((2,)),
            dma((n_heads, 2, half)), dma((n_heads, 2, half)),
            dma((n_heads, 2, half)), dma((n_heads, 2, half)),
            dma((n_heads,)), dma((n_heads,)), dma((n_heads,)),
            dma((n_heads, 2)), dma((n_heads, 2)), dma((n_heads, 2)),
            dma((n_s,)), dma((n_s,)), dma((n_t,)), dma((n_t,)),
        ],
        compiler_params=pltpu.CompilerParams(
            collective_id=0, has_side_effects=True, vmem_limit_bytes=40 * 2**20),
        name="ring_attention",
    )(slab_order, doc_lengths, sink_logit, slabs(queries), slabs(keys), slabs(values), slabs(grad_out))
    return (gq.reshape(queries.shape), gk.reshape(keys.shape), gv.reshape(values.shape), gs)


def solution(mesh):
    rows = P("dp", "ctx", None)
    return jax.shard_map(
        functools.partial(on_device, mesh.shape["dp"], mesh.shape["ctx"]),
        mesh=mesh,
        in_specs=(rows, rows, rows, rows, P("ctx"), P("dp", None), P("dp", None)),
        out_specs=(rows, rows, rows, P("ctx")),
        check_vma=False,
    )
```

```python
import functools
import math

import jax
import jax.numpy as jnp
from jax import lax
from jax.experimental import pallas as pl
from jax.experimental.pallas import tpu as pltpu
from jax.sharding import PartitionSpec as P

HD = 128
SLAB = 64
REACH = 4
WIN = REACH + 1
FAR = -1e30
MESH = pl.DeviceIdType.MESH
F32 = jnp.float32
BF16 = jnp.bfloat16

N_Z = 8
ARC = 6
PLACES = (0, 2, 4, 6)
UP, DOWN = 0, 1
SPARE = 3
PER_CHIP = 4
N_SLABS = N_Z * PER_CHIP
EMPTY = PER_CHIP * WIN

SENDS = {(UP, 0): 2, (UP, 2): 4, (UP, 4): 6, (DOWN, 2): 5, (DOWN, 4): 3, (DOWN, 6): 1}
GETS = {(UP, 0): 1, (UP, 2): 3, (UP, 4): 5, (DOWN, 0): 6, (DOWN, 2): 4, (DOWN, 4): 2}
GATHER_ORDER = ((DOWN, 6), (UP, 0), (DOWN, 4), (UP, 2), (DOWN, 2), (UP, 4))
REDUCE_MOST = {(UP, 0): 6, (DOWN, 4): 5, (UP, 2): 4, (DOWN, 2): 3, (UP, 4): 2, (DOWN, 0): 1}
REDUCE_ORDER = [(UP, 0, 6), (UP, 0, 5), (UP, 0, 4)]
for _d in range(6, 0, -1):
    for (_way, _b), _most in REDUCE_MOST.items():
        if _d <= _most and (_way, _b, _d) not in REDUCE_ORDER:
            REDUCE_ORDER.append((_way, _b, _d))


def facing(way, place):
    return (4 - place if way == UP else 6 - place) % 8


def kernel(n_dp, order, lens, sink, q_hbm, k_hbm, v_hbm, g_hbm,
           gq_out, gk_out, gv_out, gs_out,
           kv0, kv1, kv2, kv3, q_buf, g_buf, gq_buf, terms, part, inbox, bias, fin,
           sink_own, sink_in, gs_own, gs_in, window, slot,
           load_sem, swap_send, swap_recv, qg_load, qg_send, qg_recv, hand_send, hand_recv,
           ag_send, ag_recv, rs_send, rs_recv, gq_store, gq_send, gq_recv, back_send, back_recv,
           fin_store, fin_send, fin_recv, s_send, s_recv, t_send, t_recv):
    kvs = (kv0, kv1, kv2, kv3)
    dp, ctx = lax.axis_index("dp"), lax.axis_index("ctx")
    z, core = ctx // 2, lax.rem(ctx, 2)
    other = 1 - core
    peer = 2 * z + other
    sign = 1 - 2 * lax.rem(z + core, 2)

    def chip(distance):
        return lax.rem(z + sign * distance + 2 * N_Z, N_Z)

    up_chip, down_chip = chip(1), chip(-1)

    def head_of(of_core, place):
        flip = lax.rem(z + of_core, 2)
        return lax.rem(z - (place + flip * (5 - 2 * place)) + 2 * N_Z, N_Z)

    def device(of_chip, of_core):
        return (dp, 2 * of_chip + of_core)

    def xor(value, bit):
        return value + bit - 2 * bit * lax.rem(value // bit, 2)

    ctx_mates = [(dp, xor(ctx, bit)) for bit in (1, 2, 4, 8)]
    dp_mates = [(xor(dp, 1 << i), ctx) for i in range(n_dp.bit_length() - 1)]

    barrier = pltpu.get_barrier_semaphore()
    greeted = [device(c, k) for c in (up_chip, down_chip) for k in (core, other)]
    greeted += [ctx_mates[0], ctx_mates[2], ctx_mates[3]] + dp_mates
    for mate in greeted:
        pl.semaphore_signal(barrier, inc=1, device_id=mate, device_id_type=MESH)

    def remote(src, dst, send, recv, to):
        return pltpu.make_async_remote_copy(
            src, dst, send, recv, device_id=to, device_id_type=MESH)

    def columns(head, width):
        return pl.ds(pl.multiple_of(head * width, HD), width)

    group = q_hbm.shape[2] // k_hbm.shape[2]
    wide = group * HD
    mine = pl.ds(2 * ctx, 2)
    own_rows, other_rows = pl.ds(2 * core, 2), pl.ds(2 * other, 2)
    kv_hbm, qg_hbm, qg_buf = (k_hbm, v_hbm), (q_hbm, g_hbm), (q_buf, g_buf)

    loads = {}
    for u in (3, 0, 2, 1):
        cols = columns(head_of(core, 2 * u), HD)
        for t in range(2):
            loads[u, t] = pltpu.make_async_copy(
                kv_hbm[t].at[:, :, cols], kvs[u].at[t, mine], load_sem.at[u, t])
            loads[u, t].start()
    qg_loads = []
    for u in range(3):
        cols = columns(head_of(core, 2 * u), wide)
        for t in range(2):
            copy = pltpu.make_async_copy(
                qg_hbm[t].at[:, :, cols], qg_buf[t].at[u, own_rows], qg_load.at[u, t])
            copy.start()
            qg_loads.append(copy)
    lane = lax.broadcasted_iota(jnp.int32, (1, HD), 1)
    sink_own[...] = jnp.zeros_like(sink_own)
    sink_own[pl.ds(ctx, 1), :] = jnp.where(lane < SLAB, sink[0], sink[1])

    pl.semaphore_wait(barrier, len(greeted))

    swaps = {}
    for u in (3, 0, 2, 1):
        cols = columns(head_of(other, 2 * u), HD)
        for t in range(2):
            swaps[u, t] = remote(kv_hbm[t].at[:, :, cols], kvs[u].at[t, mine],
                                 swap_send.at[u, t], swap_recv.at[u, t], (dp, peer))
            swaps[u, t].start()

    def arrived_kv(u, t):
        theirs = pl.ds(2 * peer, 2)
        return remote(kvs[u].at[t, theirs], kvs[u].at[t, theirs],
                      swap_send.at[u, t], swap_recv.at[u, t], (dp, peer))

    def chip_rows(of_chip):
        return pl.ds(PER_CHIP * of_chip, PER_CHIP)

    def gather(way, place, step):
        source = chip_rows(chip(1 - step if way == UP else step - 1))
        to = facing(way, place)
        return remote(
            kvs[place // 2].at[:, source], kvs[to // 2].at[:, source],
            ag_send.at[place // 2, way, step - 1], ag_recv.at[to // 2, 1 - way, step - 1],
            device((up_chip, down_chip)[way], core))

    def gathered(way, place, step):
        source = chip_rows(chip(-step if way == UP else step))
        here = kvs[place // 2].at[:, source]
        return remote(here, here, ag_send.at[place // 2, way, step - 1],
                      ag_recv.at[place // 2, way, step - 1], (dp, peer))

    class Exchange:
        def __init__(self, own, slots, send, recv, mates):
            self.own, self.slots, self.send, self.recv = own, slots, send, recv
            self.todo = list(enumerate(mates))
            self.going = None

        def step(self):
            if self.going is not None:
                at, copy = self.going
                copy.wait()
                self.own[...] = self.own[...] + self.slots[at]
                self.going = None
            if self.todo:
                at, mate = self.todo.pop(0)
                copy = remote(self.own, self.slots.at[at], self.send.at[at], self.recv.at[at], mate)
                copy.start()
                self.going = (at, copy)

        def finish(self):
            while self.todo or self.going is not None:
                self.step()

    for way, place in GATHER_ORDER:
        u = place // 2
        if (u, 0) in loads:
            for t in range(2):
                loads.pop((u, t)).wait()
                arrived_kv(u, t).wait_recv()
        gather(way, place, 1).start()

    qg_swaps = []
    for u in range(3):
        cols = columns(head_of(other, 2 * u), wide)
        for t in range(2):
            copy = remote(qg_hbm[t].at[:, :, cols], qg_buf[t].at[u, own_rows],
                          qg_send.at[u, t], qg_recv.at[u, t], (dp, peer))
            copy.start()
            qg_swaps.append(copy)

    def arrived_qg(u, t):
        there = qg_buf[t].at[u, other_rows]
        return remote(there, there, qg_send.at[u, t], qg_recv.at[u, t], (dp, peer))

    def hand(rel, t):
        of_core, to = ((core, down_chip), (other, up_chip))[rel]
        cols = columns(head_of(of_core, 6), wide)
        return remote(qg_hbm[t].at[:, :, cols], qg_buf[t].at[SPARE, own_rows],
                      hand_send.at[rel, t], hand_recv.at[rel, t], device(to, of_core))

    def handed(rel, t):
        there = qg_buf[t].at[SPARE, (own_rows, other_rows)[rel]]
        return remote(there, there, hand_send.at[rel, t], hand_recv.at[rel, t], (dp, peer))

    row = lax.rem(lane, SLAB)
    key = lax.broadcasted_iota(jnp.int32, (WIN * SLAB, HD), 0)
    for e, of_chip in enumerate((z, down_chip)):
        places = [order[0, PER_CHIP * of_chip + i] for i in range(PER_CHIP)]

        def note_slab(j, carry, e=e, places=places):
            place = order[0, j]
            new = []
            for i in range(PER_CHIP):
                w = place - places[i] + REACH
                slot[(e * N_SLABS + j) * PER_CHIP + i] = jnp.where(
                    (w >= 0) & (w < WIN), i * WIN + w, EMPTY)
                for v in range(WIN):
                    new.append(jnp.where(w == v, j, carry[i * WIN + v]))
            return tuple(new)

        found = lax.fori_loop(0, N_SLABS, note_slab, (jnp.int32(0),) * EMPTY)
        for i in range(EMPTY):
            window[e * EMPTY + i] = found[i]
        for i in range(PER_CHIP):
            here = places[i] * SLAB + row
            begin = jnp.zeros_like(here)
            end = jnp.int32(0)
            for d in range(lens.shape[1]):
                end = end + lens[0, d]
                begin = jnp.where(here >= end, end, begin)
            begin = begin - (places[i] - REACH) * SLAB
            allowed = (key >= begin) & (key <= row + REACH * SLAB)
            bias[e, i] = jnp.where(allowed, 0.0, FAR)
    for u in range(4):
        terms[u, EMPTY] = jnp.zeros_like(terms[u, EMPTY])
    gs_own[...] = jnp.zeros_like(gs_own)

    factor = 1.0 / math.sqrt(HD)
    pairs = group // 2

    def attend(u, e, i):
        unit = SPARE if e else u
        kv = kvs[u]
        at = [window[e * EMPTY + i * WIN + w] for w in range(WIN)]
        keys = jnp.concatenate([kv[0, at[w]] for w in range(WIN)], axis=0)
        vals = jnp.concatenate([kv[1, at[w]] for w in range(WIN)], axis=0)
        q = jnp.concatenate([q_buf[unit, i, :, h * HD:(h + 1) * HD] for h in range(group)], axis=0)
        g = jnp.concatenate([g_buf[unit, i, :, h * HD:(h + 1) * HD] for h in range(group)], axis=0)
        first = pairs * head_of(core, 2 * u)
        sinks = jnp.concatenate([sink_own[pl.ds(first + p, 1), :] for p in range(pairs)], axis=1)
        nt = (((1,), (1,)), ((), ()))
        scores = lax.dot_general(keys, q, nt, preferred_element_type=F32)
        grad_prob = lax.dot_general(vals, g, nt, preferred_element_type=F32)
        scores = scores * factor + jnp.concatenate([bias[e, i]] * pairs, axis=1)
        peak = jnp.maximum(sinks, jnp.max(scores, axis=0, keepdims=True))
        weights = jnp.exp(scores - peak)
        sink_weight = jnp.exp(sinks - peak)
        total = sink_weight + jnp.sum(weights, axis=0, keepdims=True)
        inverse = 1.0 / total
        softmax = weights * inverse
        rounded = softmax.astype(BF16)
        delta = jnp.sum(rounded.astype(F32) * grad_prob, axis=0, keepdims=True)
        grad_score = (softmax * (grad_prob - delta)).astype(BF16)
        grad_key = jnp.dot(grad_score, q, preferred_element_type=F32) * factor
        grad_val = jnp.dot(rounded, g, preferred_element_type=F32)
        grad_query = lax.dot_general(
            grad_score, keys, (((0,), (0,)), ((), ())), preferred_element_type=F32) * factor
        for h in range(group):
            gq_buf[unit, i, :, h * HD:(h + 1) * HD] = grad_query[h * SLAB:(h + 1) * SLAB].astype(BF16)
        for w in range(WIN):
            terms[unit, i * WIN + w, 0] = grad_key[w * SLAB:(w + 1) * SLAB]
            terms[unit, i * WIN + w, 1] = grad_val[w * SLAB:(w + 1) * SLAB]
        share = sink_weight * inverse * delta
        for p in range(pairs):
            where = pl.ds(first + p, 1)
            gs_own[where, :] = gs_own[where, :] - share[:, p * HD:(p + 1) * HD]

    def attend_unit(u, e):
        def one(i, carry):
            attend(u, e, i)
            return carry

        lax.fori_loop(0, PER_CHIP, one, 0)

    def gq_copies(u):
        cols = columns(head_of(core, 2 * u), wide)
        return (pltpu.make_async_copy(gq_buf.at[u, own_rows], gq_out.at[:, :, cols], gq_store.at[u]),
                remote(gq_buf.at[u, other_rows], gq_out.at[:, :, cols],
                       gq_send.at[u], gq_recv.at[u], (dp, peer)))

    def gq_arrived(u):
        there = gq_out.at[:, :, columns(head_of(other, 2 * u), wide)]
        return remote(there, there, gq_send.at[u], gq_recv.at[u], (dp, peer))

    def gq_back(rel):
        to_core = (core, other)[rel]
        return remote(gq_buf.at[SPARE, (own_rows, other_rows)[rel]],
                      gq_out.at[:, :, columns(head_of(core, 0), wide)],
                      back_send.at[rel], back_recv.at[rel], device(down_chip, to_core))

    def gq_returned(rel):
        there = gq_out.at[:, :, columns(head_of((core, other)[rel], 6), wide)]
        return remote(there, there, back_send.at[rel], back_recv.at[rel], (dp, peer))

    sinks = Exchange(sink_own, sink_in, s_send, s_recv, ctx_mates)
    for step in range(2, ARC + 1):
        sinks.step()
        for way, place in GATHER_ORDER:
            if step <= SENDS[way, place]:
                gathered(way, place, step - 1).wait_recv()
                gather(way, place, step).start()
        if step == ARC - 1:
            for rel in range(2):
                for t in range(2):
                    hand(rel, t).start()
            sinks.finish()
            for copy in qg_loads:
                copy.wait()
            for u in range(3):
                for t in range(2):
                    arrived_qg(u, t).wait_recv()
            attend_unit(1, 0)
            for copy in gq_copies(1):
                copy.start()
    attend_unit(2, 0)
    for copy in gq_copies(2):
        copy.start()
    for step in range(1, ARC + 1):
        gathered(DOWN, 0, step).wait_recv()
    attend_unit(0, 0)
    for rel in range(2):
        for t in range(2):
            handed(rel, t).wait_recv()
    attend_unit(0, 1)

    def own_terms(u, j, t):
        total = terms[u, slot[j * PER_CHIP], t]
        for i in range(1, PER_CHIP):
            total = total + terms[u, slot[j * PER_CHIP + i], t]
        if u == 0:
            for i in range(PER_CHIP):
                total = total + terms[SPARE, slot[(N_SLABS + j) * PER_CHIP + i], t]
        return total

    def reduced(n):
        way, place, d = REDUCE_ORDER[n]
        to = facing(way, place)
        return remote(part.at[n], inbox.at[to // 2, 1 - way, d - 1],
                      rs_send.at[n], rs_recv.at[to // 2, 1 - way, d - 1],
                      device((up_chip, down_chip)[way], core))

    def came_in(way, place, d):
        here = inbox.at[place // 2, way, d]
        return remote(here, here, rs_send.at[0], rs_recv.at[place // 2, way, d], (dp, peer))

    sums = Exchange(gs_own, gs_in, t_send, t_recv, ctx_mates[1:] + dp_mates + ctx_mates[:1])
    for n, (way, place, d) in enumerate(REDUCE_ORDER):
        owner = chip(d if way == UP else -d)
        first = (way, place) == (UP, 0)
        if not first:
            came_in(way, place, d).wait_recv()

        def one(j, carry, n=n, way=way, place=place, d=d, owner=owner, first=first):
            for t in range(2):
                total = own_terms(place // 2, PER_CHIP * owner + j, t)
                if not first:
                    total = total + inbox[place // 2, way, d, t, j].astype(F32)
                part[n, t, j] = total.astype(BF16)
            return carry

        lax.fori_loop(0, PER_CHIP, one, 0)
        reduced(n).start()
        if n == 2:
            for rel in range(2):
                gq_back(rel).start()
            for copy in gq_copies(0):
                copy.start()
        if n >= 2 and n % 2 == 0:
            sums.step()
    sums.finish()

    totals = gs_own[pl.ds(ctx, 1), :]
    gs_out[0] = jnp.sum(jnp.where(lane < SLAB, totals, 0.0))
    gs_out[1] = jnp.sum(jnp.where(lane < SLAB, 0.0, totals))

    gkv_out = (gk_out, gv_out)

    def fin_copies(u, t):
        cols = columns(head_of(core, 2 * u), HD)
        src = fin.at[u, t] if u < 3 else inbox.at[3, UP, 0, t]
        return (pltpu.make_async_copy(src.at[own_rows], gkv_out[t].at[:, :, cols], fin_store.at[u, t]),
                remote(src.at[other_rows], gkv_out[t].at[:, :, cols],
                       fin_send.at[u, t], fin_recv.at[u, t], (dp, peer)))

    def fin_arrived(u, t):
        there = gkv_out[t].at[:, :, columns(head_of(other, 2 * u), HD)]
        return remote(there, there, fin_send.at[u, t], fin_recv.at[u, t], (dp, peer))

    for place, ways in ((6, (UP,)), (0, (DOWN,)), (2, (UP, DOWN)), (4, (UP, DOWN))):
        u = place // 2
        for way in ways:
            came_in(way, place, 0).wait_recv()
        if u < 3:
            def last(j, carry, u=u, ways=ways):
                for t in range(2):
                    total = own_terms(u, PER_CHIP * z + j, t)
                    for way in ways:
                        total = total + inbox[u, way, 0, t, j].astype(F32)
                    fin[u, t, j] = total.astype(BF16)
                return carry

            lax.fori_loop(0, PER_CHIP, last, 0)
        for t in range(2):
            for copy in fin_copies(u, t):
                copy.start()

    for copy in list(swaps.values()) + qg_swaps:
        copy.wait_send()
    for (way, place), count in SENDS.items():
        for step in range(1, count + 1):
            gather(way, place, step).wait_send()
    for n in range(len(REDUCE_ORDER)):
        reduced(n).wait_send()
    for rel in range(2):
        for t in range(2):
            hand(rel, t).wait_send()
        gq_back(rel).wait_send()
        gq_returned(rel).wait_recv()
    for u in range(3):
        keep, away = gq_copies(u)
        keep.wait()
        away.wait_send()
        gq_arrived(u).wait_recv()
    for u in (3, 0, 1, 2):
        for t in range(2):
            keep, away = fin_copies(u, t)
            keep.wait()
            away.wait_send()
            fin_arrived(u, t).wait_recv()


def on_device(n_dp, queries, keys, values, grad_out, sink_logit, doc_lengths, slab_order):
    def slabs(x):
        return x.reshape(2, SLAB, x.shape[2])

    wide = HD * (queries.shape[2] // keys.shape[2])
    n_t = 4 + n_dp.bit_length() - 1
    n_msgs = len(REDUCE_ORDER)
    dma = pltpu.SemaphoreType.DMA
    hbm = pl.BlockSpec(memory_space=pltpu.HBM)
    any_spec = pl.BlockSpec(memory_space=pl.ANY)
    smem = pl.BlockSpec(memory_space=pltpu.SMEM)
    kv = pltpu.VMEM((2, N_SLABS, SLAB, HD), BF16)
    rows = pltpu.VMEM((4, PER_CHIP, SLAB, wide), BF16)
    gq, gk, gv, gs = pl.pallas_call(
        functools.partial(kernel, n_dp),
        out_shape=(
            jax.ShapeDtypeStruct((2, SLAB, queries.shape[2]), BF16),
            jax.ShapeDtypeStruct((2, SLAB, keys.shape[2]), BF16),
            jax.ShapeDtypeStruct((2, SLAB, keys.shape[2]), BF16),
            jax.ShapeDtypeStruct((2,), F32),
        ),
        in_specs=[smem] * 3 + [hbm] * 4,
        out_specs=(any_spec, any_spec, any_spec, smem),
        scratch_shapes=[
            kv, kv, kv, kv, rows, rows, rows,
            pltpu.VMEM((4, EMPTY + 1, 2, SLAB, HD), F32),
            pltpu.VMEM((n_msgs, 2, PER_CHIP, SLAB, HD), BF16),
            pltpu.VMEM((4, 2, ARC, 2, PER_CHIP, SLAB, HD), BF16),
            pltpu.VMEM((2, PER_CHIP, WIN * SLAB, HD), F32),
            pltpu.VMEM((3, 2, PER_CHIP, SLAB, HD), BF16),
            pltpu.VMEM((16, HD), F32),
            pltpu.VMEM((4, 16, HD), F32),
            pltpu.VMEM((16, HD), F32),
            pltpu.VMEM((n_t, 16, HD), F32),
            pltpu.SMEM((2 * EMPTY,), jnp.int32),
            pltpu.SMEM((2 * N_SLABS * PER_CHIP,), jnp.int32),
            dma((4, 2)), dma((4, 2)), dma((4, 2)),
            dma((3, 2)), dma((3, 2)), dma((3, 2)), dma((2, 2)), dma((2, 2)),
            dma((4, 2, ARC)), dma((4, 2, ARC)),
            dma((n_msgs,)), dma((4, 2, ARC)),
            dma((3,)), dma((3,)), dma((3,)), dma((2,)), dma((2,)),
            dma((4, 2)), dma((4, 2)), dma((4, 2)),
            dma((4,)), dma((4,)), dma((n_t,)), dma((n_t,)),
        ],
        compiler_params=pltpu.CompilerParams(
            collective_id=0, has_side_effects=True, vmem_limit_bytes=40 * 2**20),
        name="arc_attention",
    )(slab_order, doc_lengths, sink_logit, slabs(queries), slabs(keys), slabs(values), slabs(grad_out))
    return (gq.reshape(queries.shape), gk.reshape(keys.shape), gv.reshape(values.shape), gs)


def solution(mesh):
    rows = P("dp", "ctx", None)
    return jax.shard_map(
        functools.partial(on_device, mesh.shape["dp"]),
        mesh=mesh,
        in_specs=(rows, rows, rows, rows, P("ctx"), P("dp", None), P("dp", None)),
        out_specs=(rows, rows, rows, P("ctx")),
        check_vma=False,
    )
```

```python
import functools
import math

import jax
import jax.numpy as jnp
from jax import lax
from jax.experimental import pallas as pl
from jax.experimental.pallas import tpu as pltpu
from jax.sharding import PartitionSpec as P

HD = 128
SLAB = 64
REACH = 4
WIN = REACH + 1
FAR = -1e30
MESH = pl.DeviceIdType.MESH
F32 = jnp.float32
BF16 = jnp.bfloat16

N_Z = 8
ARC = 6
PLACES = (0, 2, 4, 6)
UP, DOWN = 0, 1
SPARE = 3
PER_CHIP = 4
N_SLABS = N_Z * PER_CHIP
EMPTY = PER_CHIP * WIN

SENDS = {(UP, 0): 2, (UP, 2): 4, (UP, 4): 6, (DOWN, 2): 5, (DOWN, 4): 3, (DOWN, 6): 1}
GETS = {(UP, 0): 1, (UP, 2): 3, (UP, 4): 5, (DOWN, 0): 6, (DOWN, 2): 4, (DOWN, 4): 2}
GATHER_ORDER = ((DOWN, 6), (UP, 0), (DOWN, 4), (UP, 2), (DOWN, 2), (UP, 4))
REDUCE_MOST = {(UP, 0): 6, (DOWN, 4): 5, (UP, 2): 4, (DOWN, 2): 3, (UP, 4): 2, (DOWN, 0): 1}
REDUCE_ORDER = [(UP, 0, 6), (UP, 0, 5), (UP, 0, 4)]
for _d in range(6, 0, -1):
    for (_way, _b), _most in REDUCE_MOST.items():
        if _d <= _most and (_way, _b, _d) not in REDUCE_ORDER:
            REDUCE_ORDER.append((_way, _b, _d))


def facing(way, place):
    return (4 - place if way == UP else 6 - place) % 8


def dp_bits(n_dp):
    bits = [1 << i for i in range(n_dp.bit_length() - 1)]
    return [part for part in (bits[:2], bits[2:]) if part]


def kernel(n_dp, order_hbm, lens_hbm, sink_hbm, q_hbm, k_hbm, v_hbm, g_hbm,
           gq_out, gk_out, gv_out, gs_out,
           kv0, kv1, kv2, kv3, q_buf, g_buf, gq_buf, terms, part, inbox, bias, fin,
           sink_own, sink_in, gs_own, gs_in, order, lens, sink, window, slot,
           small_sem, load_sem, swap_send, swap_recv, qg_load, qg_send, qg_recv, hand_send, hand_recv,
           first_send, first_recv, ag_send, ag_recv, rs_send, rs_recv, gq_store, gq_send, gq_recv, back_send, back_recv,
           fin_store, fin_send, fin_recv, s_send, s_recv, t_send, t_recv):
    kvs = (kv0, kv1, kv2, kv3)
    dp, ctx = lax.axis_index("dp"), lax.axis_index("ctx")
    z, core = ctx // 2, lax.rem(ctx, 2)
    other = 1 - core
    peer = 2 * z + other
    sign = 1 - 2 * lax.rem(z + core, 2)

    def chip(distance):
        return lax.rem(z + sign * distance + 2 * N_Z, N_Z)

    up_chip, down_chip = chip(1), chip(-1)

    def head_of(of_core, place):
        flip = lax.rem(z + of_core, 2)
        return lax.rem(z - (place + flip * (5 - 2 * place)) + 2 * N_Z, N_Z)

    def device(of_chip, of_core):
        return (dp, 2 * of_chip + of_core)

    def xor(value, bit):
        return value + bit - 2 * bit * lax.rem(value // bit, 2)

    def group(axis, bits):
        mates = []
        for pick in range(1, 1 << len(bits)):
            at = {"dp": dp, "ctx": ctx}
            for i, bit in enumerate(bits):
                if pick >> i & 1:
                    at[axis] = xor(at[axis], bit)
            mates.append((at["dp"], at["ctx"]))
        return mates

    chip_pair, far_chips = group("ctx", (1, 2)), group("ctx", (4, 8))
    dp_groups = [group("dp", bits) for bits in dp_bits(n_dp)]

    barrier = pltpu.get_barrier_semaphore()
    greeted = [device(c, k) for c in (up_chip, down_chip) for k in (core, other)]
    greeted += chip_pair[:1] + far_chips + sum(dp_groups, [])
    for mate in greeted:
        pl.semaphore_signal(barrier, inc=1, device_id=mate, device_id_type=MESH)

    def remote(src, dst, send, recv, to):
        return pltpu.make_async_remote_copy(
            src, dst, send, recv, device_id=to, device_id_type=MESH)

    def columns(head, width):
        return pl.ds(pl.multiple_of(head * width, HD), width)

    heads = q_hbm.shape[2] // k_hbm.shape[2]
    wide = heads * HD
    mine = pl.ds(2 * ctx, 2)
    own_rows, other_rows = pl.ds(2 * core, 2), pl.ds(2 * other, 2)
    kv_hbm, qg_hbm, qg_buf = (k_hbm, v_hbm), (q_hbm, g_hbm), (q_buf, g_buf)

    small = [pltpu.make_async_copy(src, dst, small_sem.at[i]) for i, (src, dst) in enumerate(
        ((order_hbm, order), (lens_hbm, lens), (sink_hbm, sink)))]
    for copy in small:
        copy.start()
    loads, swaps = [], []
    for u in range(3):
        cols = columns(head_of(core, 2 * u), HD)
        for t in range(2):
            loads.append(pltpu.make_async_copy(
                kv_hbm[t].at[:, :, cols], kvs[u].at[t, mine], load_sem.at[u, t]))
        cols = columns(head_of(core, 2 * u), wide)
        for t in range(2):
            loads.append(pltpu.make_async_copy(
                qg_hbm[t].at[:, :, cols], qg_buf[t].at[u, own_rows], qg_load.at[u, t]))

    pl.semaphore_wait(barrier, len(greeted))

    def first(way, place, rel, t):
        of_core = (core, other)[rel]
        to = facing(way, place)
        target = (up_chip, down_chip)[way ^ rel]
        return remote(
            kv_hbm[t].at[:, :, columns(head_of(of_core, place), HD)], kvs[to // 2].at[t, mine],
            first_send.at[place // 2, way, rel, t], first_recv.at[to // 2, 1 - way, rel, t],
            device(target, of_core))

    for way, place in GATHER_ORDER:
        for rel in range(2):
            for t in range(2):
                first(way, place, rel, t).start()

    for u in range(3):
        cols = columns(head_of(other, 2 * u), HD)
        for t in range(2):
            swaps.append(remote(kv_hbm[t].at[:, :, cols], kvs[u].at[t, mine],
                                swap_send.at[u, t], swap_recv.at[u, t], (dp, peer)))
        cols = columns(head_of(other, 2 * u), wide)
        for t in range(2):
            swaps.append(remote(qg_hbm[t].at[:, :, cols], qg_buf[t].at[u, own_rows],
                                qg_send.at[u, t], qg_recv.at[u, t], (dp, peer)))
    for copy in loads + swaps:
        copy.start()

    def arrived(u, t):
        theirs = kvs[u].at[t, pl.ds(2 * peer, 2)]
        there = qg_buf[t].at[u, other_rows]
        return (remote(theirs, theirs, swap_send.at[u, t], swap_recv.at[u, t], (dp, peer)),
                remote(there, there, qg_send.at[u, t], qg_recv.at[u, t], (dp, peer)))

    for copy in small:
        copy.wait()
    lane = lax.broadcasted_iota(jnp.int32, (1, HD), 1)
    sink_own[...] = jnp.zeros_like(sink_own)
    sink_own[pl.ds(ctx, 1), :] = jnp.where(lane < SLAB, sink[0, 0], sink[0, 1])

    def chip_rows(of_chip):
        return pl.ds(PER_CHIP * of_chip, PER_CHIP)

    def gather(way, place, step):
        source = chip_rows(chip(1 - step if way == UP else step - 1))
        to = facing(way, place)
        return remote(
            kvs[place // 2].at[:, source], kvs[to // 2].at[:, source],
            ag_send.at[place // 2, way, step - 1], ag_recv.at[to // 2, 1 - way, step - 1],
            device((up_chip, down_chip)[way], core))

    def wait_gathered(way, place, step):
        source = chip(-step if way == UP else step)
        if step > 1:
            here = kvs[place // 2].at[:, chip_rows(source)]
            remote(here, here, ag_send.at[place // 2, way, step - 1],
                   ag_recv.at[place // 2, way, step - 1], (dp, peer)).wait_recv()
            return
        for rel in range(2):
            for t in range(2):
                here = kvs[place // 2].at[t, pl.ds(2 * (2 * source + (core, other)[rel]), 2)]
                remote(here, here, first_send.at[place // 2, way, rel, t],
                       first_recv.at[place // 2, way, rel, t], (dp, peer)).wait_recv()

    class Exchange:
        def __init__(self, own, slots, send, recv, groups):
            self.own, self.slots, self.send, self.recv = own, slots, send, recv
            self.todo, self.used, self.going = list(groups), 0, []

        def step(self):
            if self.going:
                for _, copy in self.going:
                    copy.wait()
                values = [self.own[...]] + [self.slots[at] for at, _ in self.going]
                while len(values) > 1:
                    values = [values[i] + values[i + 1] for i in range(0, len(values), 2)]
                self.own[...] = values[0]
                self.going = []
            if self.todo:
                for mate in self.todo.pop(0):
                    at = self.used
                    copy = remote(self.own, self.slots.at[at], self.send.at[at], self.recv.at[at], mate)
                    copy.start()
                    self.going.append((at, copy))
                    self.used += 1

        def finish(self):
            while self.todo or self.going:
                self.step()

    def hand(rel, t):
        of_core, to = ((core, down_chip), (other, up_chip))[rel]
        cols = columns(head_of(of_core, 6), wide)
        return remote(qg_hbm[t].at[:, :, cols], qg_buf[t].at[SPARE, own_rows],
                      hand_send.at[rel, t], hand_recv.at[rel, t], device(to, of_core))

    def handed(rel, t):
        there = qg_buf[t].at[SPARE, (own_rows, other_rows)[rel]]
        return remote(there, there, hand_send.at[rel, t], hand_recv.at[rel, t], (dp, peer))

    row = lax.rem(lane, SLAB)
    key = lax.broadcasted_iota(jnp.int32, (WIN * SLAB, HD), 0)
    for e, of_chip in enumerate((z, down_chip)):
        places = [order[0, PER_CHIP * of_chip + i] for i in range(PER_CHIP)]

        def note_slab(j, carry, e=e, places=places):
            place = order[0, j]
            new = []
            for i in range(PER_CHIP):
                w = place - places[i] + REACH
                slot[(e * N_SLABS + j) * PER_CHIP + i] = jnp.where(
                    (w >= 0) & (w < WIN), i * WIN + w, EMPTY)
                for v in range(WIN):
                    new.append(jnp.where(w == v, j, carry[i * WIN + v]))
            return tuple(new)

        found = lax.fori_loop(0, N_SLABS, note_slab, (jnp.int32(0),) * EMPTY)
        for i in range(EMPTY):
            window[e * EMPTY + i] = found[i]
        for i in range(PER_CHIP):
            here = places[i] * SLAB + row
            begin = jnp.zeros_like(here)
            end = jnp.int32(0)
            for d in range(lens.shape[1]):
                end = end + lens[0, d]
                begin = jnp.where(here >= end, end, begin)
            begin = begin - (places[i] - REACH) * SLAB
            allowed = (key >= begin) & (key <= row + REACH * SLAB)
            bias[e, i] = jnp.where(allowed, 0.0, FAR)
    for u in range(4):
        terms[u, EMPTY] = jnp.zeros_like(terms[u, EMPTY])
    gs_own[...] = jnp.zeros_like(gs_own)

    factor = 1.0 / math.sqrt(HD)
    pairs = heads // 2

    def attend(u, e, i):
        unit = SPARE if e else u
        kv = kvs[u]
        at = [window[e * EMPTY + i * WIN + w] for w in range(WIN)]
        keys = jnp.concatenate([kv[0, at[w]] for w in range(WIN)], axis=0)
        vals = jnp.concatenate([kv[1, at[w]] for w in range(WIN)], axis=0)
        q = jnp.concatenate([q_buf[unit, i, :, h * HD:(h + 1) * HD] for h in range(heads)], axis=0)
        g = jnp.concatenate([g_buf[unit, i, :, h * HD:(h + 1) * HD] for h in range(heads)], axis=0)
        first = pairs * head_of(core, 2 * u)
        sinks = jnp.concatenate([sink_own[pl.ds(first + p, 1), :] for p in range(pairs)], axis=1)
        nt = (((1,), (1,)), ((), ()))
        scores = lax.dot_general(keys, q, nt, preferred_element_type=F32)
        grad_prob = lax.dot_general(vals, g, nt, preferred_element_type=F32)
        scores = scores * factor + jnp.concatenate([bias[e, i]] * pairs, axis=1)
        peak = jnp.maximum(sinks, jnp.max(scores, axis=0, keepdims=True))
        weights = jnp.exp(scores - peak)
        sink_weight = jnp.exp(sinks - peak)
        total = sink_weight + jnp.sum(weights, axis=0, keepdims=True)
        inverse = 1.0 / total
        softmax = weights * inverse
        rounded = softmax.astype(BF16)
        delta = jnp.sum(rounded.astype(F32) * grad_prob, axis=0, keepdims=True)
        grad_score = (softmax * (grad_prob - delta)).astype(BF16)
        grad_key = jnp.dot(grad_score, q, preferred_element_type=F32) * factor
        grad_val = jnp.dot(rounded, g, preferred_element_type=F32)
        grad_query = lax.dot_general(
            grad_score, keys, (((0,), (0,)), ((), ())), preferred_element_type=F32) * factor
        for h in range(heads):
            gq_buf[unit, i, :, h * HD:(h + 1) * HD] = grad_query[h * SLAB:(h + 1) * SLAB].astype(BF16)
        for w in range(WIN):
            terms[unit, i * WIN + w, 0] = grad_key[w * SLAB:(w + 1) * SLAB]
            terms[unit, i * WIN + w, 1] = grad_val[w * SLAB:(w + 1) * SLAB]
        share = sink_weight * inverse * delta
        for p in range(pairs):
            where = pl.ds(first + p, 1)
            gs_own[where, :] = gs_own[where, :] - share[:, p * HD:(p + 1) * HD]

    def attend_unit(u, e):
        for i in range(PER_CHIP):
            attend(u, e, i)

    def gq_copies(u):
        cols = columns(head_of(core, 2 * u), wide)
        return (pltpu.make_async_copy(gq_buf.at[u, own_rows], gq_out.at[:, :, cols], gq_store.at[u]),
                remote(gq_buf.at[u, other_rows], gq_out.at[:, :, cols],
                       gq_send.at[u], gq_recv.at[u], (dp, peer)))

    def gq_arrived(u):
        there = gq_out.at[:, :, columns(head_of(other, 2 * u), wide)]
        return remote(there, there, gq_send.at[u], gq_recv.at[u], (dp, peer))

    def gq_back(rel):
        to_core = (core, other)[rel]
        return remote(gq_buf.at[SPARE, (own_rows, other_rows)[rel]],
                      gq_out.at[:, :, columns(head_of(core, 0), wide)],
                      back_send.at[rel], back_recv.at[rel], device(down_chip, to_core))

    def gq_returned(rel):
        there = gq_out.at[:, :, columns(head_of((core, other)[rel], 6), wide)]
        return remote(there, there, back_send.at[rel], back_recv.at[rel], (dp, peer))

    sinks = Exchange(sink_own, sink_in, s_send, s_recv, [far_chips, chip_pair])
    for step in range(2, ARC + 1):
        if step in (2, 4):
            sinks.step()
        for way, place in GATHER_ORDER:
            if step <= SENDS[way, place]:
                wait_gathered(way, place, step - 1)
                gather(way, place, step).start()
        if step == ARC - 1:
            for rel in range(2):
                hand(rel, 0).start()
            sinks.finish()
            for copy in loads:
                copy.wait()
            for u in range(3):
                for t in range(2):
                    for copy in arrived(u, t):
                        copy.wait_recv()
            attend_unit(1, 0)
            for copy in gq_copies(1):
                copy.start()
    for rel in range(2):
        hand(rel, 1).start()
    attend_unit(2, 0)
    for copy in gq_copies(2):
        copy.start()
    for step in range(1, ARC + 1):
        wait_gathered(DOWN, 0, step)
    attend_unit(0, 0)
    for rel in range(2):
        for t in range(2):
            handed(rel, t).wait_recv()
    attend_unit(0, 1)

    def own_terms(u, j, t):
        total = terms[u, slot[j * PER_CHIP], t]
        for i in range(1, PER_CHIP):
            total = total + terms[u, slot[j * PER_CHIP + i], t]
        if u == 0:
            for i in range(PER_CHIP):
                total = total + terms[SPARE, slot[(N_SLABS + j) * PER_CHIP + i], t]
        return total

    def reduced(n):
        way, place, d = REDUCE_ORDER[n]
        to = facing(way, place)
        return remote(part.at[n], inbox.at[to // 2, 1 - way, d - 1],
                      rs_send.at[n], rs_recv.at[to // 2, 1 - way, d - 1],
                      device((up_chip, down_chip)[way], core))

    def came_in(way, place, d):
        here = inbox.at[place // 2, way, d]
        return remote(here, here, rs_send.at[0], rs_recv.at[place // 2, way, d], (dp, peer))

    sums = Exchange(gs_own, gs_in, t_send, t_recv, [far_chips, chip_pair] + dp_groups)
    for n, (way, place, d) in enumerate(REDUCE_ORDER):
        owner = chip(d if way == UP else -d)
        starts = (way, place) == (UP, 0)
        if not starts:
            came_in(way, place, d).wait_recv()

        def one(j, carry, n=n, way=way, place=place, d=d, owner=owner, starts=starts):
            for t in range(2):
                total = own_terms(place // 2, PER_CHIP * owner + j, t)
                if not starts:
                    total = total + inbox[place // 2, way, d, t, j].astype(F32)
                part[n, t, j] = total.astype(BF16)
            return carry

        lax.fori_loop(0, PER_CHIP, one, 0)
        reduced(n).start()
        if n == 2:
            for rel in range(2):
                gq_back(rel).start()
            for copy in gq_copies(0):
                copy.start()
        if n >= 2 and n % 4 == 2:
            sums.step()
    sums.finish()

    totals = gs_own[pl.ds(ctx, 1), :]
    gs_out[0] = jnp.sum(jnp.where(lane < SLAB, totals, 0.0))
    gs_out[1] = jnp.sum(jnp.where(lane < SLAB, 0.0, totals))

    gkv_out = (gk_out, gv_out)

    def fin_copies(u, t):
        cols = columns(head_of(core, 2 * u), HD)
        src = fin.at[u, t] if u < 3 else inbox.at[3, UP, 0, t]
        return (pltpu.make_async_copy(src.at[own_rows], gkv_out[t].at[:, :, cols], fin_store.at[u, t]),
                remote(src.at[other_rows], gkv_out[t].at[:, :, cols],
                       fin_send.at[u, t], fin_recv.at[u, t], (dp, peer)))

    def fin_arrived(u, t):
        there = gkv_out[t].at[:, :, columns(head_of(other, 2 * u), HD)]
        return remote(there, there, fin_send.at[u, t], fin_recv.at[u, t], (dp, peer))

    for place, ways in ((6, (UP,)), (0, (DOWN,)), (2, (UP, DOWN)), (4, (UP, DOWN))):
        u = place // 2
        for way in ways:
            came_in(way, place, 0).wait_recv()
        if u < 3:
            def last(j, carry, u=u, ways=ways):
                for t in range(2):
                    total = own_terms(u, PER_CHIP * z + j, t)
                    for way in ways:
                        total = total + inbox[u, way, 0, t, j].astype(F32)
                    fin[u, t, j] = total.astype(BF16)
                return carry

            lax.fori_loop(0, PER_CHIP, last, 0)
        for t in range(2):
            for copy in fin_copies(u, t):
                copy.start()

    for copy in swaps:
        copy.wait_send()
    for (way, place), count in SENDS.items():
        for rel in range(2):
            for t in range(2):
                first(way, place, rel, t).wait_send()
        for step in range(2, count + 1):
            gather(way, place, step).wait_send()
    for n in range(len(REDUCE_ORDER)):
        reduced(n).wait_send()
    for rel in range(2):
        for t in range(2):
            hand(rel, t).wait_send()
        gq_back(rel).wait_send()
        gq_returned(rel).wait_recv()
    for u in range(3):
        keep, away = gq_copies(u)
        keep.wait()
        away.wait_send()
        gq_arrived(u).wait_recv()
    for u in (3, 0, 1, 2):
        for t in range(2):
            keep, away = fin_copies(u, t)
            keep.wait()
            away.wait_send()
            fin_arrived(u, t).wait_recv()


def on_device(n_dp, queries, keys, values, grad_out, sink_logit, doc_lengths, slab_order):
    def slabs(x):
        return x.reshape(2, SLAB, x.shape[2])

    wide = HD * (queries.shape[2] // keys.shape[2])
    n_t = 6 + sum((1 << len(bits)) - 1 for bits in dp_bits(n_dp))
    n_msgs = len(REDUCE_ORDER)
    dma = pltpu.SemaphoreType.DMA
    hbm = pl.BlockSpec(memory_space=pltpu.HBM)
    any_spec = pl.BlockSpec(memory_space=pl.ANY)
    smem = pl.BlockSpec(memory_space=pltpu.SMEM)
    kv = pltpu.VMEM((2, N_SLABS, SLAB, HD), BF16)
    rows = pltpu.VMEM((4, PER_CHIP, SLAB, wide), BF16)
    gq, gk, gv, gs = pl.pallas_call(
        functools.partial(kernel, n_dp),
        out_shape=(
            jax.ShapeDtypeStruct((2, SLAB, queries.shape[2]), BF16),
            jax.ShapeDtypeStruct((2, SLAB, keys.shape[2]), BF16),
            jax.ShapeDtypeStruct((2, SLAB, keys.shape[2]), BF16),
            jax.ShapeDtypeStruct((2,), F32),
        ),
        in_specs=[hbm] * 7,
        out_specs=(any_spec, any_spec, any_spec, smem),
        scratch_shapes=[
            kv, kv, kv, kv, rows, rows, rows,
            pltpu.VMEM((4, EMPTY + 1, 2, SLAB, HD), F32),
            pltpu.VMEM((n_msgs, 2, PER_CHIP, SLAB, HD), BF16),
            pltpu.VMEM((4, 2, ARC, 2, PER_CHIP, SLAB, HD), BF16),
            pltpu.VMEM((2, PER_CHIP, WIN * SLAB, HD), F32),
            pltpu.VMEM((3, 2, PER_CHIP, SLAB, HD), BF16),
            pltpu.VMEM((16, HD), F32),
            pltpu.VMEM((6, 16, HD), F32),
            pltpu.VMEM((16, HD), F32),
            pltpu.VMEM((n_t, 16, HD), F32),
            pltpu.SMEM(slab_order.shape, jnp.int32),
            pltpu.SMEM(doc_lengths.shape, jnp.int32),
            pltpu.SMEM((1, 2), F32),
            pltpu.SMEM((2 * EMPTY,), jnp.int32),
            pltpu.SMEM((2 * N_SLABS * PER_CHIP,), jnp.int32),
            dma((3,)), dma((3, 2)), dma((3, 2)), dma((3, 2)),
            dma((3, 2)), dma((3, 2)), dma((3, 2)), dma((2, 2)), dma((2, 2)),
            dma((4, 2, 2, 2)), dma((4, 2, 2, 2)),
            dma((4, 2, ARC)), dma((4, 2, ARC)),
            dma((n_msgs,)), dma((4, 2, ARC)),
            dma((3,)), dma((3,)), dma((3,)), dma((2,)), dma((2,)),
            dma((4, 2)), dma((4, 2)), dma((4, 2)),
            dma((6,)), dma((6,)), dma((n_t,)), dma((n_t,)),
        ],
        compiler_params=pltpu.CompilerParams(
            collective_id=0, has_side_effects=True, vmem_limit_bytes=40 * 2**20),
        name="arc_attention",
    )(*[pltpu.with_memory_space_constraint(x, pltpu.HBM) for x in (
        slab_order, doc_lengths, sink_logit[None], *map(slabs, (queries, keys, values, grad_out)))])
    return (gq.reshape(queries.shape), gk.reshape(keys.shape), gv.reshape(values.shape), gs)


def solution(mesh):
    rows = P("dp", "ctx", None)
    return jax.shard_map(
        functools.partial(on_device, mesh.shape["dp"]),
        mesh=mesh,
        in_specs=(rows, rows, rows, rows, P("ctx"), P("dp", None), P("dp", None)),
        out_specs=(rows, rows, rows, P("ctx")),
        check_vma=False,
    )
```

```python
import functools
import math

import jax
import jax.numpy as jnp
from jax import lax
from jax.experimental import pallas as pl
from jax.experimental.pallas import tpu as pltpu
from jax.sharding import PartitionSpec as P

HD = 128
SLAB = 64
REACH = 4
WIN = REACH + 1
FAR = -1e30
MESH = pl.DeviceIdType.MESH
F32 = jnp.float32
BF16 = jnp.bfloat16

N_Z = 8
ARC = 6
PLACES = (0, 2, 4, 6)
UP, DOWN = 0, 1
SPARE = 3
PER_CHIP = 4
N_SLABS = N_Z * PER_CHIP
EMPTY = PER_CHIP * WIN

SENDS = {(UP, 0): 2, (UP, 2): 4, (UP, 4): 6, (DOWN, 2): 5, (DOWN, 4): 3, (DOWN, 6): 1}
GETS = {(UP, 0): 1, (UP, 2): 3, (UP, 4): 5, (DOWN, 0): 6, (DOWN, 2): 4, (DOWN, 4): 2}
GATHER_ORDER = ((DOWN, 6), (UP, 0), (DOWN, 4), (UP, 2), (DOWN, 2), (UP, 4))
REDUCE_MOST = {(UP, 0): 6, (DOWN, 4): 5, (UP, 2): 4, (DOWN, 2): 3, (UP, 4): 2, (DOWN, 0): 1}
REDUCE_ORDER = [(UP, 0, 6), (UP, 0, 5), (UP, 0, 4)]
for _d in range(6, 0, -1):
    for (_way, _b), _most in REDUCE_MOST.items():
        if _d <= _most and (_way, _b, _d) not in REDUCE_ORDER:
            REDUCE_ORDER.append((_way, _b, _d))


def facing(way, place):
    return (4 - place if way == UP else 6 - place) % 8


def dp_bits(n_dp):
    bits = [1 << i for i in range(n_dp.bit_length() - 1)]
    return [part for part in (bits[:2], bits[2:]) if part]


def kernel(n_dp, order_hbm, lens_hbm, sink_hbm, q_hbm, k_hbm, v_hbm, g_hbm,
           gq_out, gk_out, gv_out, gs_out,
           kv0, kv1, kv2, kv3, q_buf, g_buf, gq_buf, terms, ahead, rest, part, inbox, bias, fin,
           sink_own, sink_in, gs_own, gs_in, order, lens, sink, window, slot,
           hello, small_sem, load_sem, swap_send, swap_recv, qg_load, qg_send, qg_recv, hand_send, hand_recv,
           first_send, first_recv, ag_send, ag_recv, rs_send, rs_recv, gq_store, gq_send, gq_recv, back_send, back_recv,
           fin_store, fin_send, fin_recv, s_send, s_recv, t_send, t_recv):
    kvs = (kv0, kv1, kv2, kv3)
    dp, ctx = lax.axis_index("dp"), lax.axis_index("ctx")
    z, core = ctx // 2, lax.rem(ctx, 2)
    other = 1 - core
    peer = 2 * z + other
    sign = 1 - 2 * lax.rem(z + core, 2)

    def chip(distance):
        return lax.rem(z + sign * distance + 2 * N_Z, N_Z)

    up_chip, down_chip = chip(1), chip(-1)

    def head_of(of_core, place):
        flip = lax.rem(z + of_core, 2)
        return lax.rem(z - (place + flip * (5 - 2 * place)) + 2 * N_Z, N_Z)

    def device(of_chip, of_core):
        return (dp, 2 * of_chip + of_core)

    def xor(value, bit):
        return value + bit - 2 * bit * lax.rem(value // bit, 2)

    def group(axis, bits):
        mates = []
        for pick in range(1, 1 << len(bits)):
            at = {"dp": dp, "ctx": ctx}
            for i, bit in enumerate(bits):
                if pick >> i & 1:
                    at[axis] = xor(at[axis], bit)
            mates.append((at["dp"], at["ctx"]))
        return mates

    chip_pair, far_chips = group("ctx", (1, 2)), group("ctx", (4, 8))
    dp_groups = [group("dp", bits) for bits in dp_bits(n_dp)]

    dp_mates = []
    for mates in dp_groups:
        for pick, mate in enumerate(mates, 1):
            dp_mates.append((mate, jnp.where(mate[0] > dp, 1, 0)))
    higher = sum([above for _, above in dp_mates], jnp.int32(0))
    barrier = pltpu.get_barrier_semaphore()
    greeted = [device(c, k) for c in (up_chip, down_chip) for k in (core, other)]
    greeted += chip_pair[:1] + far_chips
    for mate in greeted:
        pl.semaphore_signal(barrier, inc=1, device_id=mate, device_id_type=MESH)
    for mate, above in dp_mates:
        @pl.when(above == 1)
        def _(mate=mate):
            pl.semaphore_signal(barrier, inc=1, device_id=mate, device_id_type=MESH)

    def remote(src, dst, send, recv, to):
        return pltpu.make_async_remote_copy(
            src, dst, send, recv, device_id=to, device_id_type=MESH)

    def columns(head, width):
        return pl.ds(pl.multiple_of(head * width, HD), width)

    heads = q_hbm.shape[2] // k_hbm.shape[2]
    wide = heads * HD
    mine = pl.ds(2 * ctx, 2)
    own_rows, other_rows = pl.ds(2 * core, 2), pl.ds(2 * other, 2)
    kv_hbm, qg_hbm, qg_buf = (k_hbm, v_hbm), (q_hbm, g_hbm), (q_buf, g_buf)

    small = [pltpu.make_async_copy(src, dst, small_sem.at[i]) for i, (src, dst) in enumerate(
        ((order_hbm, order), (lens_hbm, lens), (sink_hbm, sink)))]
    for copy in small:
        copy.start()
    loads, swaps = [], []
    for u in range(3):
        cols = columns(head_of(core, 2 * u), HD)
        for t in range(2):
            loads.append(pltpu.make_async_copy(
                kv_hbm[t].at[:, :, cols], kvs[u].at[t, mine], load_sem.at[u, t]))
        cols = columns(head_of(core, 2 * u), wide)
        for t in range(2):
            loads.append(pltpu.make_async_copy(
                qg_hbm[t].at[:, :, cols], qg_buf[t].at[u, own_rows], qg_load.at[u, t]))

    pl.semaphore_wait(barrier, len(greeted) + len(dp_mates) - higher)
    for mate, above in dp_mates:
        @pl.when(above == 0)
        def _(mate=mate):
            pl.semaphore_signal(hello, inc=1, device_id=mate, device_id_type=MESH)

    def first(way, place, rel, t):
        of_core = (core, other)[rel]
        to = facing(way, place)
        target = (up_chip, down_chip)[way ^ rel]
        return remote(
            kv_hbm[t].at[:, :, columns(head_of(of_core, place), HD)], kvs[to // 2].at[t, mine],
            first_send.at[place // 2, way, rel, t], first_recv.at[to // 2, 1 - way, rel, t],
            device(target, of_core))

    for way, place in GATHER_ORDER:
        for rel in range(2):
            for t in range(2):
                first(way, place, rel, t).start()

    for u in range(3):
        cols = columns(head_of(other, 2 * u), HD)
        for t in range(2):
            swaps.append(remote(kv_hbm[t].at[:, :, cols], kvs[u].at[t, mine],
                                swap_send.at[u, t], swap_recv.at[u, t], (dp, peer)))
        cols = columns(head_of(other, 2 * u), wide)
        for t in range(2):
            swaps.append(remote(qg_hbm[t].at[:, :, cols], qg_buf[t].at[u, own_rows],
                                qg_send.at[u, t], qg_recv.at[u, t], (dp, peer)))
    for copy in loads + swaps:
        copy.start()

    def arrived(u, t):
        theirs = kvs[u].at[t, pl.ds(2 * peer, 2)]
        there = qg_buf[t].at[u, other_rows]
        return (remote(theirs, theirs, swap_send.at[u, t], swap_recv.at[u, t], (dp, peer)),
                remote(there, there, qg_send.at[u, t], qg_recv.at[u, t], (dp, peer)))

    for copy in small:
        copy.wait()
    lane = lax.broadcasted_iota(jnp.int32, (1, HD), 1)
    sink_own[...] = jnp.zeros_like(sink_own)
    sink_own[pl.ds(ctx, 1), :] = jnp.where(lane < SLAB, sink[0, 0], sink[0, 1])

    def chip_rows(of_chip):
        return pl.ds(PER_CHIP * of_chip, PER_CHIP)

    def gather(way, place, step):
        source = chip_rows(chip(1 - step if way == UP else step - 1))
        to = facing(way, place)
        return remote(
            kvs[place // 2].at[:, source], kvs[to // 2].at[:, source],
            ag_send.at[place // 2, way, step - 1], ag_recv.at[to // 2, 1 - way, step - 1],
            device((up_chip, down_chip)[way], core))

    def wait_gathered(way, place, step):
        source = chip(-step if way == UP else step)
        if step > 1:
            here = kvs[place // 2].at[:, chip_rows(source)]
            remote(here, here, ag_send.at[place // 2, way, step - 1],
                   ag_recv.at[place // 2, way, step - 1], (dp, peer)).wait_recv()
            return
        for rel in range(2):
            for t in range(2):
                here = kvs[place // 2].at[t, pl.ds(2 * (2 * source + (core, other)[rel]), 2)]
                remote(here, here, first_send.at[place // 2, way, rel, t],
                       first_recv.at[place // 2, way, rel, t], (dp, peer)).wait_recv()

    class Exchange:
        def __init__(self, own, slots, send, recv, groups):
            self.own, self.slots, self.send, self.recv = own, slots, send, recv
            self.todo, self.used, self.going = list(groups), 0, []

        def step(self):
            if self.going:
                for _, copy in self.going:
                    copy.wait()
                values = [self.own[...]] + [self.slots[at] for at, _ in self.going]
                while len(values) > 1:
                    values = [values[i] + values[i + 1] for i in range(0, len(values), 2)]
                self.own[...] = values[0]
                self.going = []
            if self.todo:
                for mate in self.todo.pop(0):
                    at = self.used
                    copy = remote(self.own, self.slots.at[at], self.send.at[at], self.recv.at[at], mate)
                    copy.start()
                    self.going.append((at, copy))
                    self.used += 1

        def finish(self):
            while self.todo or self.going:
                self.step()

    def hand(rel, t):
        of_core, to = ((core, down_chip), (other, up_chip))[rel]
        cols = columns(head_of(of_core, 6), wide)
        return remote(qg_hbm[t].at[:, :, cols], qg_buf[t].at[SPARE, own_rows],
                      hand_send.at[rel, t], hand_recv.at[rel, t], device(to, of_core))

    def handed(rel, t):
        there = qg_buf[t].at[SPARE, (own_rows, other_rows)[rel]]
        return remote(there, there, hand_send.at[rel, t], hand_recv.at[rel, t], (dp, peer))

    row = lax.rem(lane, SLAB)
    key = lax.broadcasted_iota(jnp.int32, (WIN * SLAB, HD), 0)
    for e, of_chip in enumerate((z, down_chip)):
        places = [order[0, PER_CHIP * of_chip + i] for i in range(PER_CHIP)]

        def note_slab(j, carry, e=e, places=places):
            place = order[0, j]
            new = []
            for i in range(PER_CHIP):
                w = place - places[i] + REACH
                slot[(e * N_SLABS + j) * PER_CHIP + i] = jnp.where(
                    (w >= 0) & (w < WIN), i * WIN + w, EMPTY)
                for v in range(WIN):
                    new.append(jnp.where(w == v, j, carry[i * WIN + v]))
            return tuple(new)

        found = lax.fori_loop(0, N_SLABS, note_slab, (jnp.int32(0),) * EMPTY)
        for i in range(EMPTY):
            window[e * EMPTY + i] = found[i]
        for i in range(PER_CHIP):
            here = places[i] * SLAB + row
            begin = jnp.zeros_like(here)
            end = jnp.int32(0)
            for d in range(lens.shape[1]):
                end = end + lens[0, d]
                begin = jnp.where(here >= end, end, begin)
            begin = begin - (places[i] - REACH) * SLAB
            allowed = (key >= begin) & (key <= row + REACH * SLAB)
            bias[e, i] = jnp.where(allowed, 0.0, FAR)
    for u in range(4):
        terms[u, EMPTY] = jnp.zeros_like(terms[u, EMPTY])
    gs_own[...] = jnp.zeros_like(gs_own)

    factor = 1.0 / math.sqrt(HD)
    pairs = heads // 2

    nt = (((1,), (1,)), ((), ()))

    def scores_of(u, e, i):
        unit = SPARE if e else u
        at = [window[e * EMPTY + i * WIN + w] for w in range(WIN)]
        keys = jnp.concatenate([kvs[u][0, at[w]] for w in range(WIN)], axis=0)
        vals = jnp.concatenate([kvs[u][1, at[w]] for w in range(WIN)], axis=0)
        q = jnp.concatenate([q_buf[unit, i, :, h * HD:(h + 1) * HD] for h in range(heads)], axis=0)
        g = jnp.concatenate([g_buf[unit, i, :, h * HD:(h + 1) * HD] for h in range(heads)], axis=0)
        scores = lax.dot_general(keys, q, nt, preferred_element_type=F32)
        grad_prob = lax.dot_general(vals, g, nt, preferred_element_type=F32)
        return keys, q, g, scores, grad_prob

    def softmax_of(u, e, i, scores, grad_prob):
        first = pairs * head_of(core, 2 * u)
        sinks = jnp.concatenate([sink_own[pl.ds(first + p, 1), :] for p in range(pairs)], axis=1)
        scores = scores * factor + jnp.concatenate([bias[e, i]] * pairs, axis=1)
        peak = jnp.maximum(sinks, jnp.max(scores, axis=0, keepdims=True))
        weights = jnp.exp(scores - peak)
        sink_weight = jnp.exp(sinks - peak)
        total = sink_weight + jnp.sum(weights, axis=0, keepdims=True)
        inverse = 1.0 / total
        softmax = weights * inverse
        rounded = softmax.astype(BF16)
        delta = jnp.sum(rounded.astype(F32) * grad_prob, axis=0, keepdims=True)
        grad_score = (softmax * (grad_prob - delta)).astype(BF16)
        share = sink_weight * inverse * delta
        for p in range(pairs):
            where = pl.ds(first + p, 1)
            gs_own[where, :] = gs_own[where, :] - share[:, p * HD:(p + 1) * HD]
        return rounded, grad_score

    def grads_of(u, e, i, keys, q, g, rounded, grad_score):
        unit = SPARE if e else u
        grad_key = jnp.dot(grad_score, q, preferred_element_type=F32) * factor
        grad_val = jnp.dot(rounded, g, preferred_element_type=F32)
        grad_query = lax.dot_general(
            grad_score, keys, (((0,), (0,)), ((), ())), preferred_element_type=F32) * factor
        for h in range(heads):
            gq_buf[unit, i, :, h * HD:(h + 1) * HD] = grad_query[h * SLAB:(h + 1) * SLAB].astype(BF16)
        for w in range(WIN):
            terms[unit, i * WIN + w, 0] = grad_key[w * SLAB:(w + 1) * SLAB]
            terms[unit, i * WIN + w, 1] = grad_val[w * SLAB:(w + 1) * SLAB]

    def attend_unit(u, e):
        made = [scores_of(u, e, i) for i in range(PER_CHIP)]
        probs = [softmax_of(u, e, i, *made[i][3:]) for i in range(PER_CHIP)]
        for i in range(PER_CHIP):
            grads_of(u, e, i, *made[i][:3], *probs[i])

    def gq_copies(u):
        cols = columns(head_of(core, 2 * u), wide)
        return (pltpu.make_async_copy(gq_buf.at[u, own_rows], gq_out.at[:, :, cols], gq_store.at[u]),
                remote(gq_buf.at[u, other_rows], gq_out.at[:, :, cols],
                       gq_send.at[u], gq_recv.at[u], (dp, peer)))

    def gq_arrived(u):
        there = gq_out.at[:, :, columns(head_of(other, 2 * u), wide)]
        return remote(there, there, gq_send.at[u], gq_recv.at[u], (dp, peer))

    def gq_back(rel):
        to_core = (core, other)[rel]
        return remote(gq_buf.at[SPARE, (own_rows, other_rows)[rel]],
                      gq_out.at[:, :, columns(head_of(core, 0), wide)],
                      back_send.at[rel], back_recv.at[rel], device(down_chip, to_core))

    def gq_returned(rel):
        there = gq_out.at[:, :, columns(head_of((core, other)[rel], 6), wide)]
        return remote(there, there, back_send.at[rel], back_recv.at[rel], (dp, peer))

    sinks = Exchange(sink_own, sink_in, s_send, s_recv, [far_chips, chip_pair])
    for step in range(2, ARC + 1):
        if step in (2, 4):
            sinks.step()
        for way, place in GATHER_ORDER:
            if step <= SENDS[way, place]:
                wait_gathered(way, place, step - 1)
                gather(way, place, step).start()
        if step == ARC - 1:
            for rel in range(2):
                hand(rel, 0).start()
            sinks.finish()
            for copy in loads:
                copy.wait()
            for u in range(3):
                for t in range(2):
                    for copy in arrived(u, t):
                        copy.wait_recv()
            attend_unit(1, 0)
            for copy in gq_copies(1):
                copy.start()
    for rel in range(2):
        hand(rel, 1).start()
    attend_unit(2, 0)
    for copy in gq_copies(2):
        copy.start()
    for step in range(1, ARC + 1):
        wait_gathered(DOWN, 0, step)
    attend_unit(0, 0)
    for rel in range(2):
        for t in range(2):
            handed(rel, t).wait_recv()
    attend_unit(0, 1)

    def own_terms(u, j, t):
        total = terms[u, slot[j * PER_CHIP], t]
        for i in range(1, PER_CHIP):
            total = total + terms[u, slot[j * PER_CHIP + i], t]
        if u == 0:
            for i in range(PER_CHIP):
                total = total + terms[SPARE, slot[(N_SLABS + j) * PER_CHIP + i], t]
        return total

    def reduced(n):
        way, place, d = REDUCE_ORDER[n]
        to = facing(way, place)
        return remote(part.at[n], inbox.at[to // 2, 1 - way, d - 1],
                      rs_send.at[n], rs_recv.at[to // 2, 1 - way, d - 1],
                      device((up_chip, down_chip)[way], core))

    def came_in(way, place, d):
        here = inbox.at[place // 2, way, d]
        return remote(here, here, rs_send.at[0], rs_recv.at[place // 2, way, d], (dp, peer))

    sums = Exchange(gs_own, gs_in, t_send, t_recv, [far_chips, chip_pair] + dp_groups)
    for n, (way, place, d) in enumerate(REDUCE_ORDER):
        owner = chip(d if way == UP else -d)
        starts = (way, place) == (UP, 0)

        def own(j, carry, n=n, place=place, owner=owner, starts=starts):
            for t in range(2):
                total = own_terms(place // 2, PER_CHIP * owner + j, t)
                if starts:
                    part[n, t, j] = total.astype(BF16)
                else:
                    ahead[t, j] = total
            return carry

        def add(j, carry, n=n, way=way, place=place, d=d):
            for t in range(2):
                part[n, t, j] = (ahead[t, j] + inbox[place // 2, way, d, t, j].astype(F32)).astype(BF16)
            return carry

        lax.fori_loop(0, PER_CHIP, own, 0)
        if not starts:
            came_in(way, place, d).wait_recv()
            lax.fori_loop(0, PER_CHIP, add, 0)
        reduced(n).start()
        if n == 2:
            for rel in range(2):
                gq_back(rel).start()
            for copy in gq_copies(0):
                copy.start()
        if n == 10 and dp_mates:
            @pl.when(higher > 0)
            def _():
                pl.semaphore_wait(hello, higher)
        if n >= 2 and n % 4 == 2:
            sums.step()
    for u in range(3):
        def own_rest(j, carry, u=u):
            for t in range(2):
                rest[u, t, j] = own_terms(u, PER_CHIP * z + j, t)
            return carry

        lax.fori_loop(0, PER_CHIP, own_rest, 0)
    sums.finish()

    totals = gs_own[pl.ds(ctx, 1), :]
    gs_out[0] = jnp.sum(jnp.where(lane < SLAB, totals, 0.0))
    gs_out[1] = jnp.sum(jnp.where(lane < SLAB, 0.0, totals))

    gkv_out = (gk_out, gv_out)

    def fin_copies(u, t):
        cols = columns(head_of(core, 2 * u), HD)
        src = fin.at[u, t] if u < 3 else inbox.at[3, UP, 0, t]
        return (pltpu.make_async_copy(src.at[own_rows], gkv_out[t].at[:, :, cols], fin_store.at[u, t]),
                remote(src.at[other_rows], gkv_out[t].at[:, :, cols],
                       fin_send.at[u, t], fin_recv.at[u, t], (dp, peer)))

    def fin_arrived(u, t):
        there = gkv_out[t].at[:, :, columns(head_of(other, 2 * u), HD)]
        return remote(there, there, fin_send.at[u, t], fin_recv.at[u, t], (dp, peer))

    for place, ways in ((6, (UP,)), (0, (DOWN,)), (2, (UP, DOWN)), (4, (UP, DOWN))):
        u = place // 2
        for way in ways:
            came_in(way, place, 0).wait_recv()
        if u < 3:
            def last(j, carry, u=u, ways=ways):
                for t in range(2):
                    total = rest[u, t, j]
                    for way in ways:
                        total = total + inbox[u, way, 0, t, j].astype(F32)
                    fin[u, t, j] = total.astype(BF16)
                return carry

            lax.fori_loop(0, PER_CHIP, last, 0)
        for t in range(2):
            for copy in fin_copies(u, t):
                copy.start()

    for copy in swaps:
        copy.wait_send()
    for (way, place), count in SENDS.items():
        for rel in range(2):
            for t in range(2):
                first(way, place, rel, t).wait_send()
        for step in range(2, count + 1):
            gather(way, place, step).wait_send()
    for n in range(len(REDUCE_ORDER)):
        reduced(n).wait_send()
    for rel in range(2):
        for t in range(2):
            hand(rel, t).wait_send()
        gq_back(rel).wait_send()
        gq_returned(rel).wait_recv()
    for u in range(3):
        keep, away = gq_copies(u)
        keep.wait()
        away.wait_send()
        gq_arrived(u).wait_recv()
    for u in (3, 0, 1, 2):
        for t in range(2):
            keep, away = fin_copies(u, t)
            keep.wait()
            away.wait_send()
            fin_arrived(u, t).wait_recv()


def on_device(n_dp, queries, keys, values, grad_out, sink_logit, doc_lengths, slab_order):
    def slabs(x):
        return x.reshape(2, SLAB, x.shape[2])

    wide = HD * (queries.shape[2] // keys.shape[2])
    n_t = 6 + sum((1 << len(bits)) - 1 for bits in dp_bits(n_dp))
    n_msgs = len(REDUCE_ORDER)
    dma = pltpu.SemaphoreType.DMA
    hbm = pl.BlockSpec(memory_space=pltpu.HBM)
    any_spec = pl.BlockSpec(memory_space=pl.ANY)
    smem = pl.BlockSpec(memory_space=pltpu.SMEM)
    kv = pltpu.VMEM((2, N_SLABS, SLAB, HD), BF16)
    rows = pltpu.VMEM((4, PER_CHIP, SLAB, wide), BF16)
    gq, gk, gv, gs = pl.pallas_call(
        functools.partial(kernel, n_dp),
        out_shape=(
            jax.ShapeDtypeStruct((2, SLAB, queries.shape[2]), BF16),
            jax.ShapeDtypeStruct((2, SLAB, keys.shape[2]), BF16),
            jax.ShapeDtypeStruct((2, SLAB, keys.shape[2]), BF16),
            jax.ShapeDtypeStruct((2,), F32),
        ),
        in_specs=[hbm] * 7,
        out_specs=(any_spec, any_spec, any_spec, smem),
        scratch_shapes=[
            kv, kv, kv, kv, rows, rows, rows,
            pltpu.VMEM((4, EMPTY + 1, 2, SLAB, HD), F32),
            pltpu.VMEM((2, PER_CHIP, SLAB, HD), F32),
            pltpu.VMEM((3, 2, PER_CHIP, SLAB, HD), F32),
            pltpu.VMEM((n_msgs, 2, PER_CHIP, SLAB, HD), BF16),
            pltpu.VMEM((4, 2, ARC, 2, PER_CHIP, SLAB, HD), BF16),
            pltpu.VMEM((2, PER_CHIP, WIN * SLAB, HD), F32),
            pltpu.VMEM((3, 2, PER_CHIP, SLAB, HD), BF16),
            pltpu.VMEM((16, HD), F32),
            pltpu.VMEM((6, 16, HD), F32),
            pltpu.VMEM((16, HD), F32),
            pltpu.VMEM((n_t, 16, HD), F32),
            pltpu.SMEM(slab_order.shape, jnp.int32),
            pltpu.SMEM(doc_lengths.shape, jnp.int32),
            pltpu.SMEM((1, 2), F32),
            pltpu.SMEM((2 * EMPTY,), jnp.int32),
            pltpu.SMEM((2 * N_SLABS * PER_CHIP,), jnp.int32),
            pltpu.SemaphoreType.REGULAR,
            dma((3,)), dma((3, 2)), dma((3, 2)), dma((3, 2)),
            dma((3, 2)), dma((3, 2)), dma((3, 2)), dma((2, 2)), dma((2, 2)),
            dma((4, 2, 2, 2)), dma((4, 2, 2, 2)),
            dma((4, 2, ARC)), dma((4, 2, ARC)),
            dma((n_msgs,)), dma((4, 2, ARC)),
            dma((3,)), dma((3,)), dma((3,)), dma((2,)), dma((2,)),
            dma((4, 2)), dma((4, 2)), dma((4, 2)),
            dma((6,)), dma((6,)), dma((n_t,)), dma((n_t,)),
        ],
        compiler_params=pltpu.CompilerParams(
            collective_id=0, has_side_effects=True, vmem_limit_bytes=40 * 2**20),
        name="arc_attention",
    )(*[pltpu.with_memory_space_constraint(x, pltpu.HBM) for x in (
        slab_order, doc_lengths, sink_logit[None], *map(slabs, (queries, keys, values, grad_out)))])
    return (gq.reshape(queries.shape), gk.reshape(keys.shape), gv.reshape(values.shape), gs)


def solution(mesh):
    rows = P("dp", "ctx", None)
    return jax.shard_map(
        functools.partial(on_device, mesh.shape["dp"]),
        mesh=mesh,
        in_specs=(rows, rows, rows, rows, P("ctx"), P("dp", None), P("dp", None)),
        out_specs=(rows, rows, rows, P("ctx")),
        check_vma=False,
    )
```

```python
import functools
import math

import jax
import jax.numpy as jnp
from jax import lax
from jax.experimental import pallas as pl
from jax.experimental.pallas import tpu as pltpu
from jax.sharding import PartitionSpec as P

HD = 128
SLAB = 64
REACH = 4
WIN = REACH + 1
FAR = -1e30
MESH = pl.DeviceIdType.MESH
F32 = jnp.float32
BF16 = jnp.bfloat16

N_Z = 8
ARC = 6
PLACES = (0, 2, 4, 6)
UP, DOWN = 0, 1
SPARE = 3
PER_CHIP = 4
N_SLABS = N_Z * PER_CHIP
EMPTY = PER_CHIP * WIN
EARLY = 10

SENDS = {(UP, 0): 2, (UP, 2): 4, (UP, 4): 6, (DOWN, 2): 5, (DOWN, 4): 3, (DOWN, 6): 1}
GETS = {(UP, 0): 1, (UP, 2): 3, (UP, 4): 5, (DOWN, 0): 6, (DOWN, 2): 4, (DOWN, 4): 2}
GATHER_ORDER = ((DOWN, 6), (UP, 0), (DOWN, 4), (UP, 2), (DOWN, 2), (UP, 4))
REDUCE_MOST = {(UP, 0): 6, (DOWN, 4): 5, (UP, 2): 4, (DOWN, 2): 3, (UP, 4): 2, (DOWN, 0): 1}
REDUCE_ORDER = [(UP, 0, 6), (UP, 0, 5), (UP, 0, 4)]
for _d in range(6, 0, -1):
    for (_way, _b), _most in REDUCE_MOST.items():
        if _d <= _most and (_way, _b, _d) not in REDUCE_ORDER:
            REDUCE_ORDER.append((_way, _b, _d))


def facing(way, place):
    return (4 - place if way == UP else 6 - place) % 8


def dp_bits(n_dp):
    bits = [1 << i for i in range(n_dp.bit_length() - 1)]
    return [part for part in (bits[:2], bits[2:]) if part]


def kernel(n_dp, order_hbm, lens_hbm, sink_hbm, q_hbm, k_hbm, v_hbm, g_hbm,
           gq_out, gk_out, gv_out, gs_out,
           kv0, kv1, kv2, kv3, q_buf, g_buf, gq_buf, terms, ahead, rest, part, inbox, bias, fin,
           sink_own, sink_in, gs_own, gs_in, order, lens, sink, window, slot,
           hello, far_hello, small_sem, load_sem, swap_send, swap_recv, qg_load, qg_send, qg_recv, hand_send, hand_recv,
           first_send, first_recv, ag_send, ag_recv, rs_send, rs_recv, gq_store, gq_send, gq_recv, back_send, back_recv,
           fin_store, fin_send, fin_recv, s_send, s_recv, t_send, t_recv):
    kvs = (kv0, kv1, kv2, kv3)
    dp, ctx = lax.axis_index("dp"), lax.axis_index("ctx")
    z, core = ctx // 2, lax.rem(ctx, 2)
    other = 1 - core
    peer = 2 * z + other
    sign = 1 - 2 * lax.rem(z + core, 2)

    def chip(distance):
        return lax.rem(z + sign * distance + 2 * N_Z, N_Z)

    up_chip, down_chip = chip(1), chip(-1)

    def head_of(of_core, place):
        flip = lax.rem(z + of_core, 2)
        return lax.rem(z - (place + flip * (5 - 2 * place)) + 2 * N_Z, N_Z)

    def device(of_chip, of_core):
        return (dp, 2 * of_chip + of_core)

    def xor(value, bit):
        return value + bit - 2 * bit * lax.rem(value // bit, 2)

    def group(axis, bits):
        mates = []
        for pick in range(1, 1 << len(bits)):
            at = {"dp": dp, "ctx": ctx}
            for i, bit in enumerate(bits):
                if pick >> i & 1:
                    at[axis] = xor(at[axis], bit)
            mates.append((at["dp"], at["ctx"]))
        return mates

    chip_pair, far_chips = group("ctx", (1, 2)), group("ctx", (4, 8))
    dp_groups = [group("dp", bits) for bits in dp_bits(n_dp)]

    dp_mates = []
    for mates in dp_groups:
        for pick, mate in enumerate(mates, 1):
            dp_mates.append((mate, jnp.where(mate[0] > dp, 1, 0)))
    far_mates = [(mate, jnp.where(mate[1] > ctx, 1, 0)) for mate in far_chips]
    higher = sum([above for _, above in dp_mates], jnp.int32(0))
    far_higher = sum([above for _, above in far_mates], jnp.int32(0))
    barrier = pltpu.get_barrier_semaphore()
    greeted = [device(c, k) for c in (up_chip, down_chip) for k in (core, other)]
    greeted += chip_pair[:1]
    for mate in greeted:
        pl.semaphore_signal(barrier, inc=1, device_id=mate, device_id_type=MESH)
    for mate, above in far_mates + dp_mates:
        @pl.when(above == 1)
        def _(mate=mate):
            pl.semaphore_signal(barrier, inc=1, device_id=mate, device_id_type=MESH)

    def remote(src, dst, send, recv, to):
        return pltpu.make_async_remote_copy(
            src, dst, send, recv, device_id=to, device_id_type=MESH)

    def columns(head, width):
        return pl.ds(pl.multiple_of(head * width, HD), width)

    heads = q_hbm.shape[2] // k_hbm.shape[2]
    wide = heads * HD
    mine = pl.ds(2 * ctx, 2)
    own_rows, other_rows = pl.ds(2 * core, 2), pl.ds(2 * other, 2)
    kv_hbm, qg_hbm, qg_buf = (k_hbm, v_hbm), (q_hbm, g_hbm), (q_buf, g_buf)

    small = [pltpu.make_async_copy(src, dst, small_sem.at[i]) for i, (src, dst) in enumerate(
        ((order_hbm, order), (lens_hbm, lens), (sink_hbm, sink)))]
    for copy in small:
        copy.start()
    loads, swaps = [], []
    for u in range(3):
        cols = columns(head_of(core, 2 * u), HD)
        for t in range(2):
            loads.append(pltpu.make_async_copy(
                kv_hbm[t].at[:, :, cols], kvs[u].at[t, mine], load_sem.at[u, t]))
        cols = columns(head_of(core, 2 * u), wide)
        for t in range(2):
            loads.append(pltpu.make_async_copy(
                qg_hbm[t].at[:, :, cols], qg_buf[t].at[u, own_rows], qg_load.at[u, t]))

    others = len(far_mates) + len(dp_mates) - far_higher - higher
    pl.semaphore_wait(barrier, len(greeted) + others)

    def first(way, place, rel, t):
        of_core = (core, other)[rel]
        to = facing(way, place)
        target = (up_chip, down_chip)[way ^ rel]
        return remote(
            kv_hbm[t].at[:, :, columns(head_of(of_core, place), HD)], kvs[to // 2].at[t, mine],
            first_send.at[place // 2, way, rel, t], first_recv.at[to // 2, 1 - way, rel, t],
            device(target, of_core))

    for way, place in GATHER_ORDER:
        for rel in range(2):
            for t in range(2):
                first(way, place, rel, t).start()

    for back, mates in ((far_hello, far_mates), (hello, dp_mates)):
        for mate, above in mates:
            @pl.when(above == 0)
            def _(mate=mate, back=back):
                pl.semaphore_signal(back, inc=1, device_id=mate, device_id_type=MESH)

    for u in range(3):
        cols = columns(head_of(other, 2 * u), HD)
        for t in range(2):
            swaps.append(remote(kv_hbm[t].at[:, :, cols], kvs[u].at[t, mine],
                                swap_send.at[u, t], swap_recv.at[u, t], (dp, peer)))
        cols = columns(head_of(other, 2 * u), wide)
        for t in range(2):
            swaps.append(remote(qg_hbm[t].at[:, :, cols], qg_buf[t].at[u, own_rows],
                                qg_send.at[u, t], qg_recv.at[u, t], (dp, peer)))
    for copy in loads + swaps:
        copy.start()

    def arrived(u, t):
        theirs = kvs[u].at[t, pl.ds(2 * peer, 2)]
        there = qg_buf[t].at[u, other_rows]
        return (remote(theirs, theirs, swap_send.at[u, t], swap_recv.at[u, t], (dp, peer)),
                remote(there, there, qg_send.at[u, t], qg_recv.at[u, t], (dp, peer)))

    for copy in small:
        copy.wait()
    lane = lax.broadcasted_iota(jnp.int32, (1, HD), 1)
    sink_own[...] = jnp.zeros_like(sink_own)
    sink_own[pl.ds(ctx, 1), :] = jnp.where(lane < SLAB, sink[0, 0], sink[0, 1])

    def chip_rows(of_chip):
        return pl.ds(PER_CHIP * of_chip, PER_CHIP)

    def gather(way, place, step):
        source = chip_rows(chip(1 - step if way == UP else step - 1))
        to = facing(way, place)
        return remote(
            kvs[place // 2].at[:, source], kvs[to // 2].at[:, source],
            ag_send.at[place // 2, way, step - 1], ag_recv.at[to // 2, 1 - way, step - 1],
            device((up_chip, down_chip)[way], core))

    def wait_gathered(way, place, step):
        source = chip(-step if way == UP else step)
        if step > 1:
            here = kvs[place // 2].at[:, chip_rows(source)]
            remote(here, here, ag_send.at[place // 2, way, step - 1],
                   ag_recv.at[place // 2, way, step - 1], (dp, peer)).wait_recv()
            return
        for rel in range(2):
            for t in range(2):
                here = kvs[place // 2].at[t, pl.ds(2 * (2 * source + (core, other)[rel]), 2)]
                remote(here, here, first_send.at[place // 2, way, rel, t],
                       first_recv.at[place // 2, way, rel, t], (dp, peer)).wait_recv()

    class Exchange:
        def __init__(self, own, slots, send, recv, groups):
            self.own, self.slots, self.send, self.recv = own, slots, send, recv
            self.todo, self.used, self.going = list(groups), 0, []

        def step(self):
            if self.going:
                for _, copy in self.going:
                    copy.wait()
                values = [self.own[...]] + [self.slots[at] for at, _ in self.going]
                while len(values) > 1:
                    values = [values[i] + values[i + 1] for i in range(0, len(values), 2)]
                self.own[...] = values[0]
                self.going = []
            if self.todo:
                for mate in self.todo.pop(0):
                    at = self.used
                    copy = remote(self.own, self.slots.at[at], self.send.at[at], self.recv.at[at], mate)
                    copy.start()
                    self.going.append((at, copy))
                    self.used += 1

        def finish(self):
            while self.todo or self.going:
                self.step()

    def hand(rel, t):
        of_core, to = ((core, down_chip), (other, up_chip))[rel]
        cols = columns(head_of(of_core, 6), wide)
        return remote(qg_hbm[t].at[:, :, cols], qg_buf[t].at[SPARE, own_rows],
                      hand_send.at[rel, t], hand_recv.at[rel, t], device(to, of_core))

    def handed(rel, t):
        there = qg_buf[t].at[SPARE, (own_rows, other_rows)[rel]]
        return remote(there, there, hand_send.at[rel, t], hand_recv.at[rel, t], (dp, peer))

    row = lax.rem(lane, SLAB)
    key = lax.broadcasted_iota(jnp.int32, (WIN * SLAB, HD), 0)
    for e, of_chip in enumerate((z, down_chip)):
        places = [order[0, PER_CHIP * of_chip + i] for i in range(PER_CHIP)]

        def note_slab(j, carry, e=e, places=places):
            place = order[0, j]
            new = []
            for i in range(PER_CHIP):
                w = place - places[i] + REACH
                slot[(e * N_SLABS + j) * PER_CHIP + i] = jnp.where(
                    (w >= 0) & (w < WIN), i * WIN + w, EMPTY)
                for v in range(WIN):
                    new.append(jnp.where(w == v, j, carry[i * WIN + v]))
            return tuple(new)

        found = lax.fori_loop(0, N_SLABS, note_slab, (jnp.int32(0),) * EMPTY)
        for i in range(EMPTY):
            window[e * EMPTY + i] = found[i]
        for i in range(PER_CHIP):
            here = places[i] * SLAB + row
            begin = jnp.zeros_like(here)
            end = jnp.int32(0)
            for d in range(lens.shape[1]):
                end = end + lens[0, d]
                begin = jnp.where(here >= end, end, begin)
            begin = begin - (places[i] - REACH) * SLAB
            allowed = (key >= begin) & (key <= row + REACH * SLAB)
            bias[e, i] = jnp.where(allowed, 0.0, FAR)
    for u in range(4):
        terms[u, EMPTY] = jnp.zeros_like(terms[u, EMPTY])
    gs_own[...] = jnp.zeros_like(gs_own)

    factor = 1.0 / math.sqrt(HD)
    pairs = heads // 2

    nt = (((1,), (1,)), ((), ()))

    def scores_of(u, e, i):
        unit = SPARE if e else u
        at = [window[e * EMPTY + i * WIN + w] for w in range(WIN)]
        keys = jnp.concatenate([kvs[u][0, at[w]] for w in range(WIN)], axis=0)
        vals = jnp.concatenate([kvs[u][1, at[w]] for w in range(WIN)], axis=0)
        q = jnp.concatenate([q_buf[unit, i, :, h * HD:(h + 1) * HD] for h in range(heads)], axis=0)
        g = jnp.concatenate([g_buf[unit, i, :, h * HD:(h + 1) * HD] for h in range(heads)], axis=0)
        scores = lax.dot_general(keys, q, nt, preferred_element_type=F32)
        grad_prob = lax.dot_general(vals, g, nt, preferred_element_type=F32)
        return keys, q, g, scores, grad_prob

    def softmax_of(u, e, i, scores, grad_prob):
        first = pairs * head_of(core, 2 * u)
        sinks = jnp.concatenate([sink_own[pl.ds(first + p, 1), :] for p in range(pairs)], axis=1)
        scores = scores * factor + jnp.concatenate([bias[e, i]] * pairs, axis=1)
        peak = jnp.maximum(sinks, jnp.max(scores, axis=0, keepdims=True))
        weights = jnp.exp(scores - peak)
        sink_weight = jnp.exp(sinks - peak)
        total = sink_weight + jnp.sum(weights, axis=0, keepdims=True)
        inverse = 1.0 / total
        softmax = weights * inverse
        rounded = softmax.astype(BF16)
        delta = jnp.sum(rounded.astype(F32) * grad_prob, axis=0, keepdims=True)
        grad_score = (softmax * (grad_prob - delta)).astype(BF16)
        share = sink_weight * inverse * delta
        for p in range(pairs):
            where = pl.ds(first + p, 1)
            gs_own[where, :] = gs_own[where, :] - share[:, p * HD:(p + 1) * HD]
        return rounded, grad_score

    def grads_of(u, e, i, keys, q, g, rounded, grad_score):
        unit = SPARE if e else u
        grad_key = jnp.dot(grad_score, q, preferred_element_type=F32) * factor
        grad_val = jnp.dot(rounded, g, preferred_element_type=F32)
        grad_query = lax.dot_general(
            grad_score, keys, (((0,), (0,)), ((), ())), preferred_element_type=F32) * factor
        for h in range(heads):
            gq_buf[unit, i, :, h * HD:(h + 1) * HD] = grad_query[h * SLAB:(h + 1) * SLAB].astype(BF16)
        for w in range(WIN):
            terms[unit, i * WIN + w, 0] = grad_key[w * SLAB:(w + 1) * SLAB]
            terms[unit, i * WIN + w, 1] = grad_val[w * SLAB:(w + 1) * SLAB]

    def attend_unit(u, e):
        made = [scores_of(u, e, i) for i in range(PER_CHIP)]
        probs = [softmax_of(u, e, i, *made[i][3:]) for i in range(PER_CHIP)]
        for i in range(PER_CHIP):
            grads_of(u, e, i, *made[i][:3], *probs[i])

    def gq_copies(u):
        cols = columns(head_of(core, 2 * u), wide)
        return (pltpu.make_async_copy(gq_buf.at[u, own_rows], gq_out.at[:, :, cols], gq_store.at[u]),
                remote(gq_buf.at[u, other_rows], gq_out.at[:, :, cols],
                       gq_send.at[u], gq_recv.at[u], (dp, peer)))

    def gq_arrived(u):
        there = gq_out.at[:, :, columns(head_of(other, 2 * u), wide)]
        return remote(there, there, gq_send.at[u], gq_recv.at[u], (dp, peer))

    def gq_back(rel):
        to_core = (core, other)[rel]
        return remote(gq_buf.at[SPARE, (own_rows, other_rows)[rel]],
                      gq_out.at[:, :, columns(head_of(core, 0), wide)],
                      back_send.at[rel], back_recv.at[rel], device(down_chip, to_core))

    def gq_returned(rel):
        there = gq_out.at[:, :, columns(head_of((core, other)[rel], 6), wide)]
        return remote(there, there, back_send.at[rel], back_recv.at[rel], (dp, peer))

    sinks = Exchange(sink_own, sink_in, s_send, s_recv, [far_chips, chip_pair])
    for step in range(2, ARC + 1):
        if step == 3:
            @pl.when(far_higher > 0)
            def _():
                pl.semaphore_wait(far_hello, far_higher)
        if step in (3, 4):
            sinks.step()
        for way, place in GATHER_ORDER:
            if step <= SENDS[way, place]:
                wait_gathered(way, place, step - 1)
                gather(way, place, step).start()
        if step == ARC - 1:
            for rel in range(2):
                hand(rel, 0).start()
            sinks.finish()
            for copy in loads:
                copy.wait()
            for u in range(3):
                for t in range(2):
                    for copy in arrived(u, t):
                        copy.wait_recv()
            attend_unit(1, 0)
            for copy in gq_copies(1):
                copy.start()
    for rel in range(2):
        hand(rel, 1).start()
    attend_unit(2, 0)
    for copy in gq_copies(2):
        copy.start()
    for step in range(1, ARC + 1):
        wait_gathered(DOWN, 0, step)
    attend_unit(0, 0)
    for rel in range(2):
        for t in range(2):
            handed(rel, t).wait_recv()
    attend_unit(0, 1)

    def own_terms(u, j, t):
        total = terms[u, slot[j * PER_CHIP], t]
        for i in range(1, PER_CHIP):
            total = total + terms[u, slot[j * PER_CHIP + i], t]
        if u == 0:
            for i in range(PER_CHIP):
                total = total + terms[SPARE, slot[(N_SLABS + j) * PER_CHIP + i], t]
        return total

    def reduced(n):
        way, place, d = REDUCE_ORDER[n]
        to = facing(way, place)
        return remote(part.at[n], inbox.at[to // 2, 1 - way, d - 1],
                      rs_send.at[n], rs_recv.at[to // 2, 1 - way, d - 1],
                      device((up_chip, down_chip)[way], core))

    def came_in(way, place, d):
        here = inbox.at[place // 2, way, d]
        return remote(here, here, rs_send.at[0], rs_recv.at[place // 2, way, d], (dp, peer))

    def wait_sent():
        for copy in swaps:
            copy.wait_send()
        for (way, place), count in SENDS.items():
            for rel in range(2):
                for t in range(2):
                    first(way, place, rel, t).wait_send()
            for step in range(2, count + 1):
                gather(way, place, step).wait_send()
        for rel in range(2):
            for t in range(2):
                hand(rel, t).wait_send()

    sums = Exchange(gs_own, gs_in, t_send, t_recv, [far_chips, chip_pair] + dp_groups)
    for n, (way, place, d) in enumerate(REDUCE_ORDER):
        owner = chip(d if way == UP else -d)
        starts = (way, place) == (UP, 0)

        def own(j, carry, n=n, place=place, owner=owner, starts=starts):
            for t in range(2):
                total = own_terms(place // 2, PER_CHIP * owner + j, t)
                if starts:
                    part[n, t, j] = total.astype(BF16)
                else:
                    ahead[t, j] = total
            return carry

        def add(j, carry, n=n, way=way, place=place, d=d):
            for t in range(2):
                part[n, t, j] = (ahead[t, j] + inbox[place // 2, way, d, t, j].astype(F32)).astype(BF16)
            return carry

        lax.fori_loop(0, PER_CHIP, own, 0)
        if not starts:
            came_in(way, place, d).wait_recv()
            lax.fori_loop(0, PER_CHIP, add, 0)
        reduced(n).start()
        if n == 2:
            for rel in range(2):
                gq_back(rel).start()
            for copy in gq_copies(0):
                copy.start()
        if n == 12:
            wait_sent()
        if n == 10 and dp_mates:
            @pl.when(higher > 0)
            def _():
                pl.semaphore_wait(hello, higher)
        if n >= 2 and n % 4 == 2:
            sums.step()
    for n in range(EARLY):
        reduced(n).wait_send()
    for u in range(3):
        def own_rest(j, carry, u=u):
            for t in range(2):
                rest[u, t, j] = own_terms(u, PER_CHIP * z + j, t)
            return carry

        lax.fori_loop(0, PER_CHIP, own_rest, 0)
    sums.finish()

    totals = gs_own[pl.ds(ctx, 1), :]
    gs_out[0] = jnp.sum(jnp.where(lane < SLAB, totals, 0.0))
    gs_out[1] = jnp.sum(jnp.where(lane < SLAB, 0.0, totals))

    gkv_out = (gk_out, gv_out)

    def fin_copies(u, t):
        cols = columns(head_of(core, 2 * u), HD)
        src = fin.at[u, t] if u < 3 else inbox.at[3, UP, 0, t]
        return (pltpu.make_async_copy(src.at[own_rows], gkv_out[t].at[:, :, cols], fin_store.at[u, t]),
                remote(src.at[other_rows], gkv_out[t].at[:, :, cols],
                       fin_send.at[u, t], fin_recv.at[u, t], (dp, peer)))

    def fin_arrived(u, t):
        there = gkv_out[t].at[:, :, columns(head_of(other, 2 * u), HD)]
        return remote(there, there, fin_send.at[u, t], fin_recv.at[u, t], (dp, peer))

    for place, ways in ((2, (UP, DOWN)), (4, (DOWN, UP)), (0, (DOWN,)), (6, (UP,))):
        u = place // 2
        for way in ways:
            came_in(way, place, 0).wait_recv()
        if u < 3:
            def last(j, carry, u=u, ways=ways):
                for t in range(2):
                    total = rest[u, t, j]
                    for way in ways:
                        total = total + inbox[u, way, 0, t, j].astype(F32)
                    fin[u, t, j] = total.astype(BF16)
                return carry

            lax.fori_loop(0, PER_CHIP, last, 0)
        for t in range(2):
            for copy in fin_copies(u, t):
                copy.start()

    for n in range(EARLY, len(REDUCE_ORDER)):
        reduced(n).wait_send()
    for rel in range(2):
        gq_back(rel).wait_send()
        gq_returned(rel).wait_recv()
    for u in range(3):
        keep, away = gq_copies(u)
        keep.wait()
        away.wait_send()
        gq_arrived(u).wait_recv()
    for u in (1, 2, 0, 3):
        for t in range(2):
            keep, away = fin_copies(u, t)
            keep.wait()
            away.wait_send()
            fin_arrived(u, t).wait_recv()


def on_device(n_dp, queries, keys, values, grad_out, sink_logit, doc_lengths, slab_order):
    def slabs(x):
        return x.reshape(2, SLAB, x.shape[2])

    wide = HD * (queries.shape[2] // keys.shape[2])
    n_t = 6 + sum((1 << len(bits)) - 1 for bits in dp_bits(n_dp))
    n_msgs = len(REDUCE_ORDER)
    dma = pltpu.SemaphoreType.DMA
    hbm = pl.BlockSpec(memory_space=pltpu.HBM)
    any_spec = pl.BlockSpec(memory_space=pl.ANY)
    smem = pl.BlockSpec(memory_space=pltpu.SMEM)
    kv = pltpu.VMEM((2, N_SLABS, SLAB, HD), BF16)
    rows = pltpu.VMEM((4, PER_CHIP, SLAB, wide), BF16)
    gq, gk, gv, gs = pl.pallas_call(
        functools.partial(kernel, n_dp),
        out_shape=(
            jax.ShapeDtypeStruct((2, SLAB, queries.shape[2]), BF16),
            jax.ShapeDtypeStruct((2, SLAB, keys.shape[2]), BF16),
            jax.ShapeDtypeStruct((2, SLAB, keys.shape[2]), BF16),
            jax.ShapeDtypeStruct((2,), F32),
        ),
        in_specs=[hbm] * 7,
        out_specs=(any_spec, any_spec, any_spec, smem),
        scratch_shapes=[
            kv, kv, kv, kv, rows, rows, rows,
            pltpu.VMEM((4, EMPTY + 1, 2, SLAB, HD), F32),
            pltpu.VMEM((2, PER_CHIP, SLAB, HD), F32),
            pltpu.VMEM((3, 2, PER_CHIP, SLAB, HD), F32),
            pltpu.VMEM((n_msgs, 2, PER_CHIP, SLAB, HD), BF16),
            pltpu.VMEM((4, 2, ARC, 2, PER_CHIP, SLAB, HD), BF16),
            pltpu.VMEM((2, PER_CHIP, WIN * SLAB, HD), F32),
            pltpu.VMEM((3, 2, PER_CHIP, SLAB, HD), BF16),
            pltpu.VMEM((16, HD), F32),
            pltpu.VMEM((6, 16, HD), F32),
            pltpu.VMEM((16, HD), F32),
            pltpu.VMEM((n_t, 16, HD), F32),
            pltpu.SMEM(slab_order.shape, jnp.int32),
            pltpu.SMEM(doc_lengths.shape, jnp.int32),
            pltpu.SMEM((1, 2), F32),
            pltpu.SMEM((2 * EMPTY,), jnp.int32),
            pltpu.SMEM((2 * N_SLABS * PER_CHIP,), jnp.int32),
            pltpu.SemaphoreType.REGULAR, pltpu.SemaphoreType.REGULAR,
            dma((3,)), dma((3, 2)), dma((3, 2)), dma((3, 2)),
            dma((3, 2)), dma((3, 2)), dma((3, 2)), dma((2, 2)), dma((2, 2)),
            dma((4, 2, 2, 2)), dma((4, 2, 2, 2)),
            dma((4, 2, ARC)), dma((4, 2, ARC)),
            dma((n_msgs,)), dma((4, 2, ARC)),
            dma((3,)), dma((3,)), dma((3,)), dma((2,)), dma((2,)),
            dma((4, 2)), dma((4, 2)), dma((4, 2)),
            dma((6,)), dma((6,)), dma((n_t,)), dma((n_t,)),
        ],
        compiler_params=pltpu.CompilerParams(
            collective_id=0, has_side_effects=True, vmem_limit_bytes=40 * 2**20),
        name="arc_attention",
    )(*[pltpu.with_memory_space_constraint(x, pltpu.HBM) for x in (
        slab_order, doc_lengths, sink_logit[None], *map(slabs, (queries, keys, values, grad_out)))])
    return (gq.reshape(queries.shape), gk.reshape(keys.shape), gv.reshape(values.shape), gs)


def solution(mesh):
    rows = P("dp", "ctx", None)
    return jax.shard_map(
        functools.partial(on_device, mesh.shape["dp"]),
        mesh=mesh,
        in_specs=(rows, rows, rows, rows, P("ctx"), P("dp", None), P("dp", None)),
        out_specs=(rows, rows, rows, P("ctx")),
        check_vma=False,
    )
```
